128 devices in a mesh: row: 32 (over y, x_hi, z), col: 4 (over x_lo, core).
Axes of the slice: x: 4 (x_hi: 2, x_lo: 2; x = x_hi * 2 + x_lo), y: 4, z: 4, core: 2. Of those that a mesh axis runs over, the one named last changes fastest.
Arguments:
- factor: float32 [1, 16384, 1, 2048], P(None, 'row', None, 'col'), may hold values from -1 to 2, as said below
- adjoint: float32 [1, 16384, 1, 2048], P(None, 'row', None, 'col'), may hold values from -6 to 6
Outputs:
- updated: float32 [1, 16384, 1, 2048], P(None, 'row', None, 'col')
The draws below stay inside these ranges and needn't reach their ends.
Inputs may be any that keep to these rules, and one draw needn't show every extreme that they name: `factor`: read as the matrix L, the tiles (0, Q - 2) and (1, Q - 1) are lower triangular with diagonal entries between 1 and 2, tile (0, Q - 1) is zero, and every other tile is dense.
All inputs are finite; a program needn't handle non-finite values.
Results may differ from the reference program's by a relative error of at most 0.00011.
Values sent between devices are 32-bit elements; how exact they have to be, the bound alone decides.
No kernel may reach another device: no remote copies, remote signals or barrier semaphores. Data moves between devices by JAX's collectives and lax.ppermute only.
A program may use at most 64 MiB of HBM per device.

```python
import math
import jax
import jax.numpy as jnp
from jax import lax

BLK = 512
TROW = 1
TCOL = 1
CYCLE_ROWS = 16384
COL_SPAN = 2048
ROWS = 16384
COLS = 2048


def draw_factor(key, part):
    key = jax.random.fold_in(key, 11)
    first, second = jax.random.split(key, 2)
    noise = jax.random.normal(first, (ROWS, COLS), jnp.float32)
    noise = jnp.clip(noise, -6.0, 6.0)
    dense = jnp.clip(noise / math.sqrt(BLK), -1.0, 1.0)
    diag_values = jax.random.uniform(second, (ROWS, COLS), jnp.float32, 1.0, 2.0)
    row_ids = jnp.arange(ROWS)[:, None]
    col_ids = jnp.arange(COLS)[None, :]
    tile_row = row_ids // BLK
    tile_col = col_ids // BLK
    inner_row = row_ids % BLK
    inner_col = col_ids % BLK
    tiles = COLS // BLK
    on_diag = (tile_row == 0) & (tile_col == tiles - 2) | (tile_row == 1) & (tile_col == tiles - 1)
    upper_tile = (tile_row == 0) & (tile_col == tiles - 1)
    diag_part = jnp.where(inner_row > inner_col, 0.3 * dense, jnp.where(inner_row == inner_col, diag_values, 0.0))
    result = jnp.where(on_diag, diag_part, jnp.where(upper_tile, 0.0, dense))
    return result.reshape(TROW, CYCLE_ROWS, TCOL, COL_SPAN)


def block_levels(rng, shape, pieces, least, largest):
    def one(position, shards_of):
        draws = jax.random.uniform(jax.random.fold_in(jax.random.fold_in(rng, 6), position), (shards_of,), jnp.float32, least / len(pieces), largest / len(pieces))
        return jnp.repeat(jnp.exp(draws), shape[position] // shards_of).reshape((-1,) + (1,) * (len(shape) - position - 1))

    loudness = one(*pieces[0])
    for cut in pieces[1:]:
        loudness = loudness * one(*cut)
    return loudness


def normal_values(key, extent, spread, limit, shards=(), held_as=jnp.bfloat16):
    gain = block_levels(key, extent, shards, -0.22, 0.18) if shards else 1.0
    values = jax.random.normal(key, extent, jnp.float32) * spread * gain
    return jnp.minimum(jnp.maximum(values, -limit), limit).astype(held_as)


def setup_inputs(seed: int = 0) -> dict:
    arg_keys = jax.random.split(jax.random.key(seed), 3)
    return {
        "factor": draw_factor(jax.random.fold_in(arg_keys[2], 71), 0),
        "adjoint": normal_values(arg_keys[1], (TROW, CYCLE_ROWS, TCOL, COL_SPAN), 1.0, 6.0, ((1, 32), (3, 4)), jnp.float32),
    }


PRECISION_MAX = lax.Precision.HIGHEST

def block_adjoint(diagonal_block, diag_adj):
    product = jnp.dot(diagonal_block.T, diag_adj, precision=PRECISION_MAX)
    lower = jnp.tril(product, -1) + 0.5 * jnp.diag(jnp.diag(product))
    middle = 0.5 * (lower + lower.T)
    halfway = jax.scipy.linalg.solve_triangular(diagonal_block, middle, lower=True, trans=1)
    return jax.scipy.linalg.solve_triangular(diagonal_block, halfway.T, lower=True, trans=1)

def one_panel(matrix, adj, column_tile, diag_tile):
    col_start = column_tile * BLK
    row_start = diag_tile * BLK
    row_end = row_start + BLK
    diagonal_block = jnp.tril(matrix[row_start:row_end, col_start:col_start + BLK])
    column_multiplier = matrix[row_end:, col_start:col_start + BLK]
    col_adjoint = adj[row_end:, col_start:col_start + BLK]
    triangular_solution = jax.scipy.linalg.solve_triangular(diagonal_block, col_adjoint.T, lower=True, trans=1).T
    diag_adj = jnp.tril(adj[row_start:row_end, col_start:col_start + BLK] - jnp.dot(triangular_solution.T, column_multiplier, precision=PRECISION_MAX))
    block_adj = block_adjoint(diagonal_block, diag_adj)
    row_panel = matrix[row_start:row_end, :col_start]
    below_left = matrix[row_end:, :col_start]
    row_new = adj[row_start:row_end, :col_start] - jnp.dot(triangular_solution.T, below_left, precision=PRECISION_MAX) - 2.0 * jnp.dot(block_adj, row_panel, precision=PRECISION_MAX)
    below_new = adj[row_end:, :col_start] - jnp.dot(triangular_solution, row_panel, precision=PRECISION_MAX)
    adj = adj.at[row_end:, :col_start].set(below_new)
    adj = adj.at[row_start:row_end, :col_start].set(row_new)
    adj = adj.at[row_start:row_end, col_start:col_start + BLK].set(block_adj)
    adj = adj.at[row_end:, col_start:col_start + BLK].set(triangular_solution)
    return adj

def reference(factor, adjoint):
    matrix = factor.reshape(ROWS, COLS)
    adj = adjoint.reshape(ROWS, COLS)
    tiles = COLS // BLK
    adj = one_panel(matrix, adj, tiles - 1, 1)
    adj = one_panel(matrix, adj, tiles - 2, 0)
    return adj.reshape(factor.shape)
```

```python
import jax
import jax.numpy as jnp
from jax import lax
from jax.sharding import Mesh
from jax.sharding import PartitionSpec as P
from jax.experimental import pallas as pl
from jax.experimental.pallas import tpu as pltpu

N = 512
H = 256
ALL = ("y", "xh", "z", "xl", "core")
PLANE = ("y", "z")
F32 = jnp.float32
BF16 = jnp.bfloat16


def dev(row, column):
    return row * 4 + column


def split(x):
    hi = x.astype(BF16)
    return hi, (x - hi.astype(F32)).astype(BF16)


def as_parts(x):
    return x if isinstance(x, tuple) else split(x)


def mm(a, b, ta=False):
    ah, al = as_parts(a)
    bh, bl = as_parts(b)
    dims = (((0 if ta else 1,), (0,)), ((), ()))

    def dot(u, v):
        return lax.dot_general(u, v, dims, preferred_element_type=F32)

    return dot(ah, bh) + (dot(ah, bl) + dot(al, bh))


def mmx(a, b):
    return jnp.dot(a, b, preferred_element_type=F32, precision=lax.Precision.HIGHEST)


def iotas(n):
    return (
        lax.broadcasted_iota(jnp.int32, (n, n), 0),
        lax.broadcasted_iota(jnp.int32, (n, n), 1),
    )


def tril(x):
    i, j = iotas(x.shape[0])
    return jnp.where(i >= j, x, 0.0)


def sym_half(p):
    i, j = iotas(p.shape[0])
    low = jnp.where(i > j, p, jnp.where(i == j, 0.5 * p, 0.0))
    return 0.5 * (low + low.T)


def inverse_lower(k_ref, out_ref):
    b = 128
    i, j = iotas(b)
    blocks = [k_ref[s * b:(s + 1) * b, s * b:(s + 1) * b] for s in range(4)]
    inv = [jnp.where(i == j, 1.0 / jnp.where(i == j, t, 1.0), 0.0) for t in blocks]
    size = 1
    while size < b:
        off = (i // (2 * size) == j // (2 * size)) & (i // size > j // size)
        part = [jnp.where(off, t, 0.0) for t in blocks]
        half = [mmx(p, x) for p, x in zip(part, inv)]
        inv = [x - mmx(x, h) for x, h in zip(inv, half)]
        size *= 2
    out_ref[...] = jnp.zeros((N, N), F32)
    for s in range(4):
        out_ref[s * b:(s + 1) * b, s * b:(s + 1) * b] = inv[s]
    for s in (0, 2):
        low = k_ref[(s + 1) * b:(s + 2) * b, s * b:(s + 1) * b]
        out_ref[(s + 1) * b:(s + 2) * b, s * b:(s + 1) * b] = -mmx(inv[s + 1], mmx(low, inv[s]))
    top = out_ref[:H, :H]
    bottom = out_ref[H:, H:]
    out_ref[H:, :H] = -mmx(bottom, mmx(k_ref[H:, :H], top))


def call(kernel, outs, *args):
    vm = pl.BlockSpec(memory_space=pltpu.VMEM)
    sm = pl.BlockSpec(memory_space=pltpu.SMEM)
    return pl.pallas_call(
        kernel,
        out_shape=[jax.ShapeDtypeStruct(s, F32) for s in outs],
        in_specs=[sm if a.dtype == jnp.int32 else vm for a in args],
        out_specs=[vm for _ in outs],
        compiler_params=pltpu.CompilerParams(vmem_limit_bytes=48 * 1024 * 1024),
    )(*args)


def k_inverse(k_ref, y_ref, inv_ref, x_ref):
    inverse_lower(k_ref, inv_ref)
    x_ref[...] = mm(inv_ref[...], y_ref[...])


def k_sum_odd(pos_ref, a_ref, asw_ref, l_ref, lsw_ref, out_ref):
    row, core = pos_ref[0], pos_ref[2]
    second = core == 1
    live = row >= 2
    a3 = split(jnp.where(live, jnp.where(second, a_ref[...], asw_ref[...]), 0.0))
    a2 = split(jnp.where(live, jnp.where(second, asw_ref[...], a_ref[...]), 0.0))
    l3 = split(jnp.where(second, l_ref[:, H:], lsw_ref[:, :H]))
    l2 = split(jnp.where(second, lsw_ref[:, H:], l_ref[:, :H]))
    for t, (a, l) in enumerate(((a3, l3), (a3, l2), (a2, l2))):
        out_ref[:, t] = mm(a, l, ta=True).reshape(16, 32, H)


def k_send(pos_ref, a3_ref, a2_ref, l_ref, slice_ref, x_ref, x12_ref, out_ref):
    row, xl, core = pos_ref[0], pos_ref[1], pos_ref[2]
    zero = jnp.zeros((16, 32, N), F32)

    @pl.when(xl == 1)
    def _():
        out_ref[:, 0] = jnp.broadcast_to(slice_ref[0][None], (16, 32, N))
        out_ref[:, 1] = jnp.broadcast_to(slice_ref[1][None], (16, 32, N))

    @pl.when((xl == 0) & (row >= 2))
    def _():
        l = split(l_ref[...])
        out_ref[:, 0] = mm(a3_ref[...], l, ta=True).reshape(16, 32, N)
        out_ref[:, 1] = mm(a2_ref[...], l, ta=True).reshape(16, 32, N)

    @pl.when((xl == 0) & (row < 2))
    def _():
        out_ref[:, 0] = zero
        out_ref[:, 1] = zero

    @pl.when(row == 0)
    def _():
        out_ref[:, 2] = x_ref[...].reshape(16, 32, N)
        out_ref[:, 3] = (-mm(x12_ref[...], x_ref[...])).reshape(16, 32, N)

    @pl.when(row == 1)
    def _():
        keep = (xl == 0) | (core == 1)
        out_ref[:, 2] = zero
        out_ref[:, 3] = jnp.where(keep, x_ref[...], 0.0).reshape(16, 32, N)

    @pl.when(row >= 2)
    def _():
        out_ref[:, 2] = zero
        out_ref[:, 3] = zero


def k_second(k2_ref, i1_ref, l12_ref, i2_ref, x12_ref):
    x12_ref[...] = mm(i1_ref[...], l12_ref[...])
    inverse_lower(k2_ref, i2_ref)


def k_chain_a(t13_ref, a13_ref, i1_ref, k1_ref, sym_ref):
    g = tril(a13_ref[...] - mm(i1_ref[...], t13_ref[...], ta=True))
    sym_ref[...] = sym_half(mm(tril(k1_ref[...]), g, ta=True))


def k_chain_b(t12_ref, a12_ref, i1_ref, sym_ref, x12_ref, ap_ref):
    inner = t12_ref[...] + 2.0 * mm(sym_ref[...], x12_ref[...])
    ap_ref[...] = a12_ref[...] - mm(i1_ref[...], inner, ta=True)


def k_chain_c(t22_ref, t12_ref, a02_ref, x12_ref, ap_ref, l12_ref, i2_ref, k2_ref, sym_ref):
    inner = t22_ref[...] - mm(x12_ref[...], t12_ref[...], ta=True) + mm(ap_ref[...], l12_ref[...], ta=True)
    g = tril(a02_ref[...] - mm(i2_ref[...], inner, ta=True))
    sym_ref[...] = sym_half(mm(tril(k2_ref[...]), g, ta=True))


def k_chain_d(sym1_ref, i1_ref, sym2_ref, i2_ref, e1_ref, e2_ref):
    for s, i, e in ((sym1_ref, i1_ref, e1_ref), (sym2_ref, i2_ref, e2_ref)):
        inv = split(i[...])
        e[...] = mm(inv, mm(s[...], inv), ta=True)


def k_final(pos_ref, a_ref, a3_ref, a2_ref, got_ref, inv_ref, x_ref, x12_ref, sym_ref, ap_ref, l1_ref, e_ref, out_ref):
    row, xl, core = pos_ref[0], pos_ref[1], pos_ref[2]

    @pl.when(row >= 2)
    def _():
        base = jnp.where(xl == 0, a_ref[...], 0.0)
        m3 = got_ref[:, 3].reshape(N, N)
        m2 = got_ref[:, 2].reshape(N, N)
        out_ref[...] = base - mm(a3_ref[...], m3) - mm(a2_ref[...], m2)

    @pl.when((row == 1) & ((xl == 0) | (core == 0)))
    def _():
        m2 = got_ref[:, 2].reshape(N, N)
        out_ref[...] = -mm(ap_ref[...], m2)

    @pl.when((row == 1) & (xl == 0))
    def _():
        inner = got_ref[:, 0].reshape(N, N) + 2.0 * mm(sym_ref[...], x_ref[...])
        out_ref[...] += a_ref[...] - mm(inv_ref[...], inner, ta=True)

    @pl.when((row == 0) & (xl == 0))
    def _():
        inner = (
            got_ref[:, 1].reshape(N, N)
            - mm(x12_ref[...], got_ref[:, 0].reshape(N, N), ta=True)
            + mm(ap_ref[...], l1_ref[...], ta=True)
            + 2.0 * mm(sym_ref[...], x_ref[...])
        )
        out_ref[...] = a_ref[...] - mm(inv_ref[...], inner, ta=True)

    @pl.when((xl == 1) & (((row == 1) & (core == 1)) | ((row == 0) & (core == 0))))
    def _():
        out_ref[...] = e_ref[...]

    @pl.when((xl == 1) & (row == 0) & (core == 1))
    def _():
        out_ref[...] = a_ref[...]


def move(x, pairs):
    return lax.ppermute(x, ALL, pairs)


def exchange_cores(x, rows, columns):
    return move(x, [(dev(r, c), dev(r, c ^ 1)) for r in rows for c in columns])


def halves(x, core):
    return jnp.where(core == 0, x[:H], x[H:])


def join(mine, other, core):
    return jnp.concatenate([jnp.where(core == 0, mine, other), jnp.where(core == 0, other, mine)], 0)


def swap_xh(x):
    return lax.ppermute(x, "xh", [(0, 1), (1, 0)])


def local(factor, adjoint):
    rows = range(32)
    y, xh, z = (lax.axis_index(n) for n in ("y", "xh", "z"))
    xl, core = lax.axis_index("xl"), lax.axis_index("core")
    row = y * 8 + xh * 4 + z
    pos = jnp.stack([row, xl, core]).astype(jnp.int32)
    first, second = core == 0, core == 1
    low = factor.reshape(N, N)
    adj = adjoint.reshape(N, N)

    adj_sw = exchange_cores(adj, rows, (2, 3))
    low_sw = exchange_cores(low, rows, (2, 3))
    k_odd = jnp.where(row == 1, jnp.where(second, low, low_sw), jnp.where(first, low, low_sw))
    to_even = jnp.where(row <= 1, k_odd, adj)
    at_even = move(to_even, [(dev(r, c), dev(r, c - 2)) for r in rows for c in (2, 3)])
    at_even_sw = exchange_cores(at_even, rows, (0, 1))

    sums_odd, = call(k_sum_odd, [(16, 3, 32, H)], pos, adj, adj_sw, low, low_sw)
    got = lax.all_to_all(sums_odd, PLANE, 0, 0, tiled=True)
    part = jnp.sum(got, axis=0)
    part = part + swap_xh(part)
    odd_slice = jnp.stack([
        jnp.concatenate([part[0], part[1]], 1),
        jnp.concatenate([part[2], jnp.zeros((32, H), F32)], 1),
    ])

    eye = jnp.eye(N, dtype=F32)
    k_own = jnp.where(row <= 1, jnp.where(xl == 1, k_odd, at_even), eye)
    unit = ((row == 1) & (xl == 1) & second) | ((row == 0) & (xl == 1) & first)
    empty = (row == 0) & (xl == 1) & second
    right = jnp.where(unit, -eye, jnp.where(empty, 0.0, low))
    inv, x = call(k_inverse, [(N, N), (N, N)], k_own, right)

    from_zero = move(jnp.where(first, low, adj_sw), [(dev(0, 2), dev(1, 2)), (dev(0, 3), dev(1, 3))])
    from_zero_sw = exchange_cores(from_zero, (1,), (2, 3))
    k2 = jnp.where((row == 1) & (xl == 1), jnp.where(first, from_zero, from_zero_sw), eye)
    a02 = jnp.where(first, from_zero_sw, from_zero)
    l12 = jnp.where(first, low, low_sw)
    i2, x12 = call(k_second, [(N, N), (N, N)], k2, inv, l12)

    half = halves(x12, core)
    to_zero = move(half, [(dev(1, 2), dev(0, 0)), (dev(1, 3), dev(0, 1))])
    to_zero_odd = move(half, [(dev(1, 2), dev(0, 2)), (dev(1, 3), dev(0, 3))])
    mine = jnp.where(xl == 0, to_zero, to_zero_odd)
    x12_zero = join(mine, exchange_cores(mine, (0,), (0, 1, 2, 3)), core)
    l1_zero = move(low, [(dev(1, c), dev(0, c)) for c in (0, 1)])

    a3 = jnp.where(xl == 1, jnp.where(second, adj, adj_sw), jnp.where(second, at_even, at_even_sw))
    a2 = jnp.where(xl == 1, jnp.where(second, adj_sw, adj), jnp.where(second, at_even_sw, at_even))
    send, = call(k_send, [(16, 4, 32, N)], pos, a3, a2, low, odd_slice, x, x12_zero)
    got = lax.all_to_all(send, PLANE, 0, 0, tiled=True)
    part = jnp.sum(got, axis=0)
    part = part + swap_xh(part)

    here = got[:, :2]
    there = exchange_cores(here, (1,), (2, 3))
    left = jnp.where(first, here, there).reshape(16, 2, 32, 2, H)
    rite = jnp.where(first, there, here).reshape(16, 2, 32, 2, H)

    def tile(t):
        pick = [v[:, t // 2, :, t % 2, :].reshape(N, H) for v in (left, rite)]
        return jnp.concatenate(pick, 1)

    t13, t12, t22 = tile(0), tile(1), tile(2)
    k1 = jnp.where(second, low, low_sw)
    a13 = jnp.where(second, adj, adj_sw)
    a12 = jnp.where(second, adj_sw, adj)
    sym1, = call(k_chain_a, [(N, N)], t13, a13, inv, k1)
    ap, = call(k_chain_b, [(N, N)], t12, a12, inv, sym1, x12)
    sym2, = call(k_chain_c, [(N, N)], t22, t12, a02, x12, ap, l12, i2, k2)
    e1, e2 = call(k_chain_d, [(N, N), (N, N)], sym1, inv, sym2, i2)

    def to_even_root(v, r):
        got_half = move(halves(v, core), [(dev(1, 2), dev(r, 0)), (dev(1, 3), dev(r, 1))])
        return join(got_half, exchange_cores(got_half, (r,), (0, 1)), core)

    sym1_even = to_even_root(sym1, 1)
    ap_one = to_even_root(ap, 1)
    ap_zero = to_even_root(ap, 0)
    sym2_even = to_even_root(sym2, 0)
    e2_zero = move(e2, [(dev(1, 2), dev(0, 2))])

    got = lax.all_to_all(jnp.broadcast_to(part[None], (16, 4, 32, N)), PLANE, 0, 0, tiled=True)
    sym = jnp.where(row == 1, sym1_even, sym2_even)
    ap_here = jnp.where(xl == 1, ap, jnp.where(row == 1, ap_one, ap_zero))
    e = jnp.where(row == 1, e1, e2_zero)
    out, = call(k_final, [(N, N)], pos, adj, a3, a2, got, inv, x, x12_zero, sym, ap_here, l1_zero, e)
    return out.reshape(adjoint.shape)


def solution(mesh):
    fine = Mesh(mesh.devices.reshape(4, 2, 4, 2, 2), ALL)
    placed = P(None, ("y", "xh", "z"), None, ("xl", "core"))
    return jax.shard_map(
        local, mesh=fine, in_specs=(placed, placed), out_specs=placed, check_vma=False
    )
```

```python
import jax
import jax.numpy as jnp
from jax import lax
from jax.sharding import Mesh
from jax.sharding import PartitionSpec as P
from jax.experimental import pallas as pl
from jax.experimental.pallas import tpu as pltpu

N = 512
H = 256
ALL = ("y", "xh", "z", "xl", "core")
PLANE = ("y", "z")
F32 = jnp.float32
BF16 = jnp.bfloat16


def dev(row, column):
    return row * 4 + column


def split(x):
    hi = x.astype(BF16)
    return hi, (x - hi.astype(F32)).astype(BF16)


def as_parts(x):
    return x if isinstance(x, tuple) else split(x)


def mm(a, b, ta=False):
    ah, al = as_parts(a)
    bh, bl = as_parts(b)
    dims = (((0 if ta else 1,), (0,)), ((), ()))

    def dot(u, v):
        return lax.dot_general(u, v, dims, preferred_element_type=F32)

    return dot(ah, bh) + (dot(ah, bl) + dot(al, bh))


def iotas(n):
    return (
        lax.broadcasted_iota(jnp.int32, (n, n), 0),
        lax.broadcasted_iota(jnp.int32, (n, n), 1),
    )


def tril(x):
    i, j = iotas(x.shape[0])
    return jnp.where(i >= j, x, 0.0)


def sym_half(p):
    i, j = iotas(p.shape[0])
    low = jnp.where(i > j, p, jnp.where(i == j, 0.5 * p, 0.0))
    return 0.5 * (low + low.T)


def inverse_lower(k_ref, out_ref):
    b = 128
    i, j = iotas(b)
    inv, blocks = [], []
    for s in range(4):
        t = k_ref[s * b:(s + 1) * b, s * b:(s + 1) * b]
        on = jnp.where(i == j, t, 0.0)
        down = 1.0 / jnp.sum(on, axis=1, keepdims=True)
        across = 1.0 / jnp.sum(on, axis=0, keepdims=True)
        off = (i // 2 == j // 2) & (i > j)
        inv.append(jnp.where(i == j, down, 0.0) - jnp.where(off, down * t * across, 0.0))
        blocks.append(t)
    size = 2
    while size < b:
        off = (i // (2 * size) == j // (2 * size)) & (i // size > j // size)
        parts = [split(x) for x in inv]
        half = [mm(jnp.where(off, t, 0.0), x) for t, x in zip(blocks, parts)]
        inv = [x - mm(p, h) for x, p, h in zip(inv, parts, half)]
        size *= 2
    out_ref[...] = jnp.zeros((N, N), F32)
    for s in range(4):
        out_ref[s * b:(s + 1) * b, s * b:(s + 1) * b] = inv[s]
    for s in (0, 2):
        low = k_ref[(s + 1) * b:(s + 2) * b, s * b:(s + 1) * b]
        out_ref[(s + 1) * b:(s + 2) * b, s * b:(s + 1) * b] = -mm(inv[s + 1], mm(low, inv[s]))
    top = out_ref[:H, :H]
    bottom = out_ref[H:, H:]
    out_ref[H:, :H] = -mm(bottom, mm(k_ref[H:, :H], top))


class Bank:
    def __init__(self, buf, sem):
        self.buf, self.sem = buf, sem

    def at(self, slot):
        return self.buf.at[slot]

    def start(self, slot, src):
        pltpu.make_async_copy(flat(src), self.buf.at[slot], self.sem.at[slot]).start()

    def start_half(self, slot, src, lo):
        pltpu.make_async_copy(
            flat(src).at[:, lo:lo + H], self.buf.at[slot, :, :H], self.sem.at[slot]).start()

    def wait(self, *slots):
        for s in slots:
            pltpu.make_async_copy(self.buf.at[s], self.buf.at[s], self.sem.at[s]).wait()

    def wait_half(self, *slots):
        for s in slots:
            half = self.buf.at[s, :, :H]
            pltpu.make_async_copy(half, half, self.sem.at[s]).wait()

    def get(self, slot):
        return self.buf[slot]


def flat(ref):
    return ref.at[0, :, 0, :] if len(ref.shape) == 4 else ref


def odd_top(row, xl, core):
    return (xl == 1) & (row <= 1)


def odd_zero(row, xl, core):
    return (xl == 1) & (row == 0)


def odd_one(row, xl, core):
    return (xl == 1) & (row == 1)


LIMIT = 58 * 1024 * 1024


def call(kernel, outs, *args, slots=1, near=(), only=None):
    vm = pl.BlockSpec(memory_space=pltpu.VMEM)
    sm = pl.BlockSpec(memory_space=pltpu.SMEM)
    far = pl.BlockSpec(memory_space=pl.ANY)
    n, m = len(args), len(outs)

    def body(*refs):
        ins, out_refs, built = refs[:n], refs[n:n + m], refs[n + m:n + 2 * m]
        buf, sem, done = refs[n + 2 * m:]
        kernel(*ins, *built, buf, sem)
        copies = [pltpu.make_async_copy(b, flat(o), done.at[i]) for i, (b, o) in enumerate(zip(built, out_refs))]

        def store():
            for c in copies:
                c.start()
            for c in copies:
                c.wait()

        if only is None:
            store()
        else:
            pl.when(only(*(ins[0][i] for i in range(3))))(store)

    return pl.pallas_call(
        body,
        out_shape=[jax.ShapeDtypeStruct(s, F32) for s in outs],
        in_specs=[sm if a.dtype == jnp.int32 else vm if i in near else far for i, a in enumerate(args)],
        out_specs=[far] * m,
        scratch_shapes=[pltpu.VMEM((s[1], s[3]) if len(s) == 4 else s, F32) for s in outs] + [
            pltpu.VMEM((slots, N, N), F32), pltpu.SemaphoreType.DMA((slots,)), pltpu.SemaphoreType.DMA((m,))],
        compiler_params=pltpu.CompilerParams(vmem_limit_bytes=LIMIT),
    )(*args)


def k_sum_odd(pos_ref, a_ref, asw_ref, l_ref, lsw_ref, out_ref, buf, sem):
    row, xl, core = pos_ref[0], pos_ref[1], pos_ref[2]
    bank = Bank(buf, sem)
    live = (row >= 1) & (xl == 1)

    def begin(a3, a2, l3, l2, lo):
        bank.start(0, a3)
        bank.start_half(1, l3, lo)
        bank.start_half(2, l2, lo)
        bank.start(3, a2)

    @pl.when(live & (core == 0))
    def _():
        begin(asw_ref, a_ref, lsw_ref, l_ref, 0)

    @pl.when(live & (core == 1))
    def _():
        begin(a_ref, asw_ref, l_ref, lsw_ref, H)

    @pl.when(live)
    def _():
        bank.wait(0)
        a3 = split(jnp.where(row == 1, 0.0, bank.get(0)))
        bank.wait_half(1)
        out_ref[:, :, :H] = mm(a3, buf[1, :, :H], ta=True).reshape(16, 32, H)
        bank.wait_half(2)
        l2 = split(buf[2, :, :H])
        out_ref[:, :, H:N] = mm(a3, l2, ta=True).reshape(16, 32, H)
        bank.wait(3)
        out_ref[:, :, N:] = mm(bank.get(3), l2, ta=True).reshape(16, 32, H)

    @pl.when(jnp.logical_not(live))
    def _():
        out_ref[...] = jnp.zeros(out_ref.shape, F32)


def k_first(pos_ref, l_ref, lsw_ref, inv_ref, x12_ref, buf, sem):
    row, xl, core = pos_ref[0], pos_ref[1], pos_ref[2]
    bank = Bank(buf, sem)
    live = (xl == 1) & (row <= 1)

    @pl.when(live & (row == core))
    def _():
        bank.start(0, l_ref)
        bank.start(1, lsw_ref)

    @pl.when(live & (row != core))
    def _():
        bank.start(0, lsw_ref)
        bank.start(1, l_ref)

    @pl.when(live)
    def _():
        bank.wait(0)
        inverse_lower(bank.at(0), inv_ref)
        bank.wait(1)
        x12_ref[...] = mm(inv_ref[...], bank.get(1))


def k_second(pos_ref, l_ref, kq_ref, kqsw_ref, first_ref, x12_ref, inv_ref, x_ref, out_ref, buf, sem):
    row, xl, core = pos_ref[0], pos_ref[1], pos_ref[2]
    bank = Bank(buf, sem)
    even = (xl == 0) & (row <= 1)
    odd = (xl == 1) & (row <= 1)

    @pl.when(even & (row == core))
    def _():
        bank.start(0, kq_ref)

    @pl.when(even & (row != core))
    def _():
        bank.start(0, kqsw_ref)

    @pl.when(even)
    def _():
        bank.start(1, l_ref)

    @pl.when(even & (core == 0))
    def _():
        bank.start_half(2, kq_ref, 0)

    @pl.when(even & (core == 1))
    def _():
        bank.start_half(2, kqsw_ref, H)

    @pl.when(odd & (row == 1) & (core == 0))
    def _():
        bank.start(1, x12_ref)

    @pl.when(odd & (row == core))
    def _():
        bank.start(1, first_ref)

    @pl.when(even)
    def _():
        bank.wait(0)
        inverse_lower(bank.at(0), inv_ref)
        bank.wait(1)
        inv = split(inv_ref[...])
        x = mm(inv, bank.get(1))
        x_ref[...] = x
        out_ref[:, :, :N] = x.reshape(16, 32, N)
        bank.wait_half(2)
        half = jnp.where(row == 1, mm(inv, buf[2, :, :H]), 0.0)
        out_ref[:, :, N:] = half.reshape(16, 32, H)

    @pl.when(odd & ((row == 1) | (core == 0)))
    def _():
        bank.wait(1)
        out_ref[:, :, :N] = bank.get(1).reshape(16, 32, N)
        out_ref[:, :, N:] = jnp.zeros((16, 32, H), F32)

    @pl.when((row >= 2) | ((xl == 1) & (row == 0) & (core == 1)))
    def _():
        out_ref[...] = jnp.zeros(out_ref.shape, F32)


def k_send(pos_ref, ac_ref, acsw_ref, l_ref, part_ref, other_ref, out_ref, buf, sem):
    row, xl, core = pos_ref[0], pos_ref[1], pos_ref[2]
    bank = Bank(buf, sem)
    live = (xl == 0) & (row >= 1)

    @pl.when(live & (core == 0))
    def _():
        bank.start(0, acsw_ref)
        bank.start(2, ac_ref)

    @pl.when(live & (core == 1))
    def _():
        bank.start(0, ac_ref)
        bank.start(2, acsw_ref)

    @pl.when(live)
    def _():
        bank.start(1, l_ref)
        bank.wait(0, 1)
        l = split(bank.get(1))
        a3 = jnp.where(row == 1, 0.0, bank.get(0))
        out_ref[:, :, :N] = mm(a3, l, ta=True).reshape(16, 32, N)
        bank.wait(2)
        out_ref[:, :, N:] = mm(bank.get(2), l, ta=True).reshape(16, 32, N)

    @pl.when(xl == 1)
    def _():
        s = part_ref[...] + other_ref[...]
        out_ref[:, :, :N + H] = jnp.broadcast_to(s[None], (16, 32, N + H))
        out_ref[:, :, N + H:] = jnp.zeros((16, 32, H), F32)

    @pl.when((xl == 0) & (row == 0))
    def _():
        out_ref[...] = jnp.zeros(out_ref.shape, F32)


def k_own(got_ref, out_ref, buf, sem):
    total = got_ref[0]
    for s in range(1, 16):
        total = total + got_ref[s]
    out_ref[...] = total


def k_spread(a_ref, b_ref, out_ref, buf, sem):
    s = a_ref[...] + b_ref[...]
    out_ref[...] = jnp.broadcast_to(s[None], out_ref.shape)


def gather_tile(bank, slot, core, got_ref, gotsw_ref, lo):
    def begin(left, right):
        for half, src in ((0, left), (H, right)):
            for s in range(16):
                pltpu.make_async_copy(
                    src.at[s, :, lo:lo + H],
                    bank.buf.at[slot, s * 32:(s + 1) * 32, half:half + H],
                    bank.sem.at[slot]).start()

    @pl.when(core == 0)
    def _():
        begin(got_ref, gotsw_ref)

    @pl.when(core == 1)
    def _():
        begin(gotsw_ref, got_ref)


def k_chain_a(pos_ref, got_ref, gotsw_ref, a_ref, asw_ref, l_ref, lsw_ref, i1_ref, x12_ref, sym_ref, ap_ref, out_ref, half_ref, buf, sem):
    row, xl, core = pos_ref[0], pos_ref[1], pos_ref[2]
    bank = Bank(buf, sem)
    live = (xl == 1) & (row == 1)

    @pl.when(live)
    def _():
        gather_tile(bank, 0, core, got_ref, gotsw_ref, 0)
        bank.start(1, i1_ref)

        @pl.when(core == 0)
        def _():
            bank.start(2, asw_ref)
            bank.start(3, lsw_ref)
            bank.start(6, a_ref)

        @pl.when(core == 1)
        def _():
            bank.start(2, a_ref)
            bank.start(3, l_ref)
            bank.start(6, asw_ref)

        gather_tile(bank, 4, core, got_ref, gotsw_ref, H)
        bank.start(5, x12_ref)
        bank.wait(0, 1, 2, 3)
        i1 = split(bank.get(1))
        g = tril(bank.get(2) - mm(i1, bank.get(0), ta=True))
        sym = sym_half(mm(tril(bank.get(3)), g, ta=True))
        sym_ref[...] = sym
        bank.wait(4, 5, 6)
        inner = bank.get(4) + 2.0 * mm(sym, bank.get(5))
        ap_ref[...] = bank.get(6) - mm(i1, inner, ta=True)
        lo = pl.multiple_of(core * H, H)
        buf[4] = inner
        half_ref[...] = sym_ref[pl.ds(lo, H), :]
        out_ref[:H, :] = half_ref[...]
        out_ref[H:, :] = buf[4, pl.ds(lo, H), :]


def k_chain_b(pos_ref, got_ref, gotsw_ref, a_ref, asw_ref, l_ref, lsw_ref, i2_ref, x12_ref, x12sw_ref, half_ref, halfsw_ref, sym_ref, out_ref, buf, sem):
    row, xl, core = pos_ref[0], pos_ref[1], pos_ref[2]
    bank = Bank(buf, sem)
    live = (xl == 1) & (row == 0)

    def stack(up, down):
        pltpu.make_async_copy(up, buf.at[0, :H], sem.at[0]).start()
        pltpu.make_async_copy(down, buf.at[0, H:], sem.at[0]).start()

    @pl.when(live)
    def _():
        @pl.when(core == 0)
        def _():
            stack(half_ref, halfsw_ref)
            bank.start(1, x12_ref)

        @pl.when(core == 1)
        def _():
            stack(halfsw_ref, half_ref)
            bank.start(1, x12sw_ref)

        gather_tile(bank, 2, core, got_ref, gotsw_ref, H)
        gather_tile(bank, 3, core, got_ref, gotsw_ref, N)
        bank.start(4, i2_ref)

        @pl.when(core == 0)
        def _():
            bank.start(5, a_ref)
            bank.start(6, l_ref)

        @pl.when(core == 1)
        def _():
            bank.start(5, asw_ref)
            bank.start(6, lsw_ref)

        bank.wait(0, 1, 2)
        x12 = split(bank.get(1))
        buf[7] = bank.get(2) + 2.0 * mm(bank.get(0), x12)
        inner = mm(x12, bank.get(7), ta=True) + mm(bank.get(2), x12, ta=True)
        bank.wait(3, 4, 5, 6)
        g = tril(bank.get(5) - mm(bank.get(4), bank.get(3) - inner, ta=True))
        sym_ref[...] = sym_half(mm(tril(bank.get(6)), g, ta=True))
        lo = pl.multiple_of(core * H, H)
        out_ref[:H, :] = sym_ref[pl.ds(lo, H), :]
        out_ref[H:, :] = buf[7, pl.ds(lo, H), :]


def k_chain_c(pos_ref, sym1_ref, sym2_ref, inv_ref, e_ref, buf, sem):
    row, xl, core = pos_ref[0], pos_ref[1], pos_ref[2]
    bank = Bank(buf, sem)

    @pl.when((xl == 1) & (row == 0) & (core == 0))
    def _():
        bank.start(0, sym2_ref)

    @pl.when((xl == 1) & (row == 1) & (core == 1))
    def _():
        bank.start(0, sym1_ref)

    @pl.when((xl == 1) & (((row == 1) & (core == 1)) | ((row == 0) & (core == 0))))
    def _():
        bank.start(1, inv_ref)
        bank.wait(0, 1)
        inv = split(bank.get(1))
        e_ref[...] = mm(inv, mm(bank.get(0), inv), ta=True)


def k_final(pos_ref, a_ref, asw_ref, ac_ref, acsw_ref, xs_ref, xh_ref, inv_ref, x_ref, one_ref, onesw_ref, zero_ref, zerosw_ref, ap_ref, e_ref, *rest):
    ts_ref, res, buf, sem = rest
    row, xl, core = pos_ref[0], pos_ref[1], pos_ref[2]
    bank = Bank(buf, sem)
    X1, X2, X12, A, A3, A2 = 0, 1, 2, 3, 4, 5
    SYM, W, T, INV, XOWN, L1 = 2, 4, 5, 6, 7, 8

    def rows_of(slot, src, lo, width):
        for s in range(16):
            pltpu.make_async_copy(
                src.at[s, :, lo:lo + width], bank.buf.at[slot, s * 32:(s + 1) * 32, :width],
                bank.sem.at[slot]).start()

    def sums(slot, lo):
        rows_of(slot, ts_ref, lo, N)

    def x2(slot):
        bank.start(slot, xs_ref.at[:, :N])

    def x1(slot):
        bank.start(slot, xs_ref.at[:, N:2 * N])

    def x12(slot):
        for c, (left, right) in enumerate(((0, H), (H, 0))):
            @pl.when(core == c)
            def _():
                pltpu.make_async_copy(
                    xs_ref.at[:, 2 * N:], bank.buf.at[slot, :, left:left + H], bank.sem.at[slot]).start()
                pltpu.make_async_copy(
                    xh_ref, bank.buf.at[slot, :, right:right + H], bank.sem.at[slot]).start()

    def stack(slot, lo, here, there):
        for c, (up, down) in enumerate(((here, there), (there, here))):
            @pl.when(core == c)
            def _():
                pltpu.make_async_copy(
                    up.at[lo:lo + H], bank.buf.at[slot, :H], bank.sem.at[slot]).start()
                pltpu.make_async_copy(
                    down.at[lo:lo + H], bank.buf.at[slot, H:], bank.sem.at[slot]).start()

    low_even = (row >= 2) & (xl == 0)

    @pl.when(low_even)
    def _():
        @pl.when(core == 0)
        def _():
            bank.start(A3, acsw_ref)
            bank.start(A2, ac_ref)

        @pl.when(core == 1)
        def _():
            bank.start(A3, ac_ref)
            bank.start(A2, acsw_ref)

        x12(X12)
        x1(X1)
        x2(X2)
        bank.start(A, a_ref)
        bank.wait(A3, A2, X12)
        a3 = split(bank.get(A3))
        moved = bank.get(A2) - mm(a3, bank.get(X12))
        bank.wait(X1, A)
        res[...] = bank.get(A) - mm(a3, bank.get(X1))
        bank.wait(X2)
        res[...] -= mm(moved, bank.get(X2))

    @pl.when((row >= 2) & (xl == 1) & (core == 0))
    def _():
        bank.start(A3, asw_ref)
        x1(X1)
        bank.start(A, a_ref)
        x2(X2)
        bank.wait(A3, X1, A)
        moved = bank.get(A) - mm(bank.get(A3), bank.get(X1))
        bank.wait(X2)
        res[...] = mm(moved, bank.get(X2))

    @pl.when((row >= 2) & (xl == 1) & (core == 1))
    def _():
        bank.start(A, a_ref)
        x1(X1)
        bank.wait(A, X1)
        res[...] = mm(bank.get(A), bank.get(X1))

    @pl.when((row == 1) & (xl == 0))
    def _():
        bank.start(INV, inv_ref)

        @pl.when(core == 0)
        def _():
            bank.start(L1, ac_ref)

        @pl.when(core == 1)
        def _():
            bank.start(L1, acsw_ref)

        stack(W, H, one_ref, onesw_ref)
        x2(X2)
        stack(SYM, 0, one_ref, onesw_ref)
        bank.start(XOWN, x_ref)
        sums(T, 0)
        bank.start(A, a_ref)
        bank.wait(INV, L1, W)
        inv = split(bank.get(INV))
        ap = bank.get(L1) - mm(inv, bank.get(W), ta=True)
        bank.wait(X2)
        side = mm(ap, bank.get(X2))
        bank.wait(SYM, XOWN)
        inner = 2.0 * mm(bank.get(SYM), bank.get(XOWN))
        bank.wait(T, A)
        res[...] = bank.get(A) - side - mm(inv, inner + bank.get(T), ta=True)

    @pl.when((row == 0) & (xl == 0))
    def _():
        sums(T, 0)
        x12(L1)
        stack(W, H, zero_ref, zerosw_ref)
        x1(X1)
        stack(SYM, 0, zero_ref, zerosw_ref)
        bank.start(XOWN, x_ref)
        sums(X2, N)
        bank.start(INV, inv_ref)
        bank.start(A, a_ref)
        bank.wait(T, L1)
        inner = -mm(bank.get(L1), bank.get(T), ta=True)
        bank.wait(W, X1)
        inner = inner - mm(bank.get(W), bank.get(X1), ta=True)
        bank.wait(SYM, XOWN)
        inner = inner + 2.0 * mm(bank.get(SYM), bank.get(XOWN))
        bank.wait(X2, INV, A)
        res[...] = bank.get(A) - mm(bank.get(INV), inner + bank.get(X2), ta=True)

    @pl.when((row == 1) & (xl == 1) & (core == 0))
    def _():
        bank.start(A, ap_ref)
        x2(X2)
        bank.wait(A, X2)
        res[...] = mm(bank.get(A), bank.get(X2))

    def keep(src):
        bank.start(A, src)
        bank.wait(A)
        res[...] = bank.get(A)

    @pl.when((row == 1) & (xl == 1) & (core == 1))
    def _():
        keep(e_ref)

    @pl.when((row == 0) & (xl == 1) & (core == 0))
    def _():
        keep(e_ref)

    @pl.when((row == 0) & (xl == 1) & (core == 1))
    def _():
        keep(a_ref)


def move(x, pairs):
    return lax.ppermute(x, ALL, [(dev(*a), dev(*b)) for a, b in pairs])


def exchange_cores(x, rows, columns):
    return move(x, [((r, c), (r, c ^ 1)) for r in rows for c in columns])


def swap_xh(x):
    return lax.ppermute(x, "xh", [(0, 1), (1, 0)])


def every(x):
    return lax.all_to_all(x, PLANE, 0, 0, tiled=True)


def local(low, adj):
    rows = range(32)
    below = range(2, 32)
    y, xh, z = (lax.axis_index(n) for n in ("y", "xh", "z"))
    xl, core = lax.axis_index("xl"), lax.axis_index("core")
    pos = jnp.stack([y * 8 + xh * 4 + z, xl, core, z]).astype(jnp.int32)
    tile = (N, N)

    adj_sw = exchange_cores(adj, rows, (2, 3))
    low_sw = exchange_cores(low, rows, (2, 3))
    kq = move(low, [((1, 3), (1, 1)), ((0, 2), (0, 0)), ((1, 2), (1, 0))])
    ac = move(adj, [((r, c), (r, c - 2)) for r in below for c in (2, 3)] + [((1, 2), (1, 0))])

    sums_odd, = call(k_sum_odd, [(16, 32, N + H)], pos, adj, adj_sw, low, low_sw, slots=4)
    got = every(sums_odd)

    inv_odd, x12 = call(k_first, [tile, tile], pos, low, low_sw, slots=2, only=odd_top)
    kq_sw = exchange_cores(kq, (0, 1), (0, 1))
    inv, x, send_x = call(
        k_second, [tile, tile, (16, 32, N + H)], pos, low, kq, kq_sw, inv_odd, x12, slots=3)
    x12_zero = move(x12, [((1, 2), (0, 2))])
    x12_zero_sw = exchange_cores(x12_zero, (0,), (2,))
    got, send_x = lax.optimization_barrier((got, send_x))
    got_x = every(send_x)

    part = jnp.sum(got, axis=0)
    other = swap_xh(part)
    ac_sw = exchange_cores(ac, range(1, 32), (0, 1))
    send, = call(k_send, [(16, 32, 2 * N)], pos, ac, ac_sw, low, part, other, slots=3, near=(4, 5))
    send, got_x = lax.optimization_barrier((send, got_x))
    sums = every(send)
    xs = jnp.concatenate([got_x[0, :, :N], got_x[1]], 1)
    xs = xs + lax.ppermute(xs, "xh", [(0, 1)])
    sums, xs, x12_zero_sw = lax.optimization_barrier((sums, xs, x12_zero_sw))
    xs = lax.all_gather(xs, PLANE, tiled=True)
    sums_sw = exchange_cores(sums[:, :, :N + H], (0, 1), (2, 3))
    sym1, ap, to_one, half = call(
        k_chain_a, [tile, tile, tile, (H, N)], pos, sums, sums_sw, adj, adj_sw, low, low_sw, inv_odd, x12,
        slots=7, only=odd_one)
    sums, to_one, half = lax.optimization_barrier((sums, to_one, half))
    half = move(half, [((1, c), (0, c)) for c in (2, 3)])
    one = move(to_one, [((1, 2), (1, 0)), ((1, 3), (1, 1))])
    half_sw = exchange_cores(half, (0,), (2, 3))
    sym2, to_zero = call(
        k_chain_b, [tile, tile], pos, sums, sums_sw, adj, adj_sw, low, low_sw, inv_odd, x12_zero, x12_zero_sw,
        half, half_sw, slots=8, only=odd_zero)
    zero = move(to_zero, [((0, 2), (0, 0)), ((0, 3), (0, 1))])

    own, = call(k_own, [(32, 2 * N)], sums, near=(0,))
    send, = call(
        k_spread, [(16, 32, 2 * N)], own, lax.ppermute(own, "xh", [(1, 0)]), near=(0, 1))
    ts = every(send)

    e, = call(k_chain_c, [tile], pos, sym1, sym2, inv_odd, slots=2, only=odd_top)
    one_sw = exchange_cores(one, (1,), (0, 1))
    zero_sw = exchange_cores(zero, (0,), (0, 1))
    xs_sw = exchange_cores(xs[:, 2 * N:], rows, (0, 1))
    out, = call(
        k_final, [adj.shape], pos, adj, adj_sw, ac, ac_sw, xs, xs_sw, inv, x,
        one, one_sw, zero, zero_sw, ap, e, ts, slots=9)
    return out


def solution(mesh):
    fine = Mesh(mesh.devices.reshape(4, 2, 4, 2, 2), ALL)
    placed = P(None, ("y", "xh", "z"), None, ("xl", "core"))
    return jax.shard_map(
        local, mesh=fine, in_specs=(placed, placed), out_specs=placed, check_vma=False
    )
```

```python
import jax
import jax.numpy as jnp
from jax import lax
from jax.sharding import Mesh
from jax.sharding import PartitionSpec as P
from jax.experimental import pallas as pl
from jax.experimental.pallas import tpu as pltpu

N = 512
H = 256
ALL = ("y", "xh", "z", "xl", "core")
PLANE = ("y", "z")
F32 = jnp.float32
BF16 = jnp.bfloat16


def dev(row, column):
    return row * 4 + column


def split(x):
    hi = x.astype(BF16)
    return hi, (x - hi.astype(F32)).astype(BF16)


def as_parts(x):
    return x if isinstance(x, tuple) else split(x)


def mm(a, b, ta=False):
    ah, al = as_parts(a)
    bh, bl = as_parts(b)
    dims = (((0 if ta else 1,), (0,)), ((), ()))

    def dot(u, v):
        return lax.dot_general(u, v, dims, preferred_element_type=F32)

    return dot(ah, bh) + (dot(ah, bl) + dot(al, bh))


def iotas(n):
    return (
        lax.broadcasted_iota(jnp.int32, (n, n), 0),
        lax.broadcasted_iota(jnp.int32, (n, n), 1),
    )


def tril(x):
    i, j = iotas(x.shape[0])
    return jnp.where(i >= j, x, 0.0)


def sym_half(p):
    i, j = iotas(p.shape[0])
    low = jnp.where(i > j, p, jnp.where(i == j, 0.5 * p, 0.0))
    return 0.5 * (low + low.T)


def inverse_lower(k_ref, out_ref):
    b = 128
    i, j = iotas(b)
    inv, blocks = [], []
    for s in range(4):
        t = k_ref[s * b:(s + 1) * b, s * b:(s + 1) * b]
        on = jnp.where(i == j, t, 0.0)
        down = 1.0 / jnp.sum(on, axis=1, keepdims=True)
        across = 1.0 / jnp.sum(on, axis=0, keepdims=True)
        off = (i // 2 == j // 2) & (i > j)
        inv.append(jnp.where(i == j, down, 0.0) - jnp.where(off, down * t * across, 0.0))
        blocks.append(t)
    size = 2
    while size < b:
        off = (i // (2 * size) == j // (2 * size)) & (i // size > j // size)
        parts = [split(x) for x in inv]
        half = [mm(jnp.where(off, t, 0.0), x) for t, x in zip(blocks, parts)]
        inv = [x - mm(p, h) for x, p, h in zip(inv, parts, half)]
        size *= 2
    out_ref[...] = jnp.zeros((N, N), F32)
    for s in range(4):
        out_ref[s * b:(s + 1) * b, s * b:(s + 1) * b] = inv[s]
    for s in (0, 2):
        low = k_ref[(s + 1) * b:(s + 2) * b, s * b:(s + 1) * b]
        out_ref[(s + 1) * b:(s + 2) * b, s * b:(s + 1) * b] = -mm(inv[s + 1], mm(low, inv[s]))
    top = out_ref[:H, :H]
    bottom = out_ref[H:, H:]
    out_ref[H:, :H] = -mm(bottom, mm(k_ref[H:, :H], top))


class Bank:
    def __init__(self, buf, sem):
        self.buf, self.sem = buf, sem

    def at(self, slot):
        return self.buf.at[slot]

    def start(self, slot, src):
        pltpu.make_async_copy(flat(src), self.buf.at[slot], self.sem.at[slot]).start()

    def start_half(self, slot, src, lo):
        pltpu.make_async_copy(
            flat(src).at[:, lo:lo + H], self.buf.at[slot, :, :H], self.sem.at[slot]).start()

    def wait(self, *slots):
        for s in slots:
            pltpu.make_async_copy(self.buf.at[s], self.buf.at[s], self.sem.at[s]).wait()

    def wait_half(self, *slots):
        for s in slots:
            half = self.buf.at[s, :, :H]
            pltpu.make_async_copy(half, half, self.sem.at[s]).wait()

    def get(self, slot):
        return self.buf[slot]


def flat(ref):
    return ref.at[0, :, 0, :] if len(ref.shape) == 4 else ref


def odd_top(row, xl, core):
    return (xl == 1) & (row <= 1)


def odd_zero(row, xl, core):
    return (xl == 1) & (row == 0)


def odd_one(row, xl, core):
    return (xl == 1) & (row == 1)


LIMIT = 58 * 1024 * 1024


def call(kernel, outs, *args, slots=1, near=(), only=None):
    vm = pl.BlockSpec(memory_space=pltpu.VMEM)
    sm = pl.BlockSpec(memory_space=pltpu.SMEM)
    far = pl.BlockSpec(memory_space=pl.ANY)
    n, m = len(args), len(outs)

    def body(*refs):
        ins, out_refs, built = refs[:n], refs[n:n + m], refs[n + m:n + 2 * m]
        buf, sem, done = refs[n + 2 * m:]
        kernel(*ins, *built, buf, sem)
        copies = [pltpu.make_async_copy(b, flat(o), done.at[i]) for i, (b, o) in enumerate(zip(built, out_refs))]

        def store():
            for c in copies:
                c.start()
            for c in copies:
                c.wait()

        if only is None:
            store()
        else:
            pl.when(only(*(ins[0][i] for i in range(3))))(store)

    return pl.pallas_call(
        body,
        out_shape=[jax.ShapeDtypeStruct(s, F32) for s in outs],
        in_specs=[sm if a.dtype == jnp.int32 else vm if i in near else far for i, a in enumerate(args)],
        out_specs=[far] * m,
        scratch_shapes=[pltpu.VMEM((s[1], s[3]) if len(s) == 4 else s, F32) for s in outs] + [
            pltpu.VMEM((slots, N, N), F32), pltpu.SemaphoreType.DMA((slots,)), pltpu.SemaphoreType.DMA((m,))],
        compiler_params=pltpu.CompilerParams(vmem_limit_bytes=LIMIT),
    )(*args)


def k_sum_odd(pos_ref, a_ref, asw_ref, l_ref, lsw_ref, out_ref, buf, sem):
    row, xl, core = pos_ref[0], pos_ref[1], pos_ref[2]
    bank = Bank(buf, sem)
    live = (row >= 1) & (xl == 1)

    def begin(a3, a2, l3, l2, lo):
        bank.start(0, a3)
        bank.start_half(1, l3, lo)
        bank.start_half(2, l2, lo)
        bank.start(3, a2)

    @pl.when(live & (core == 0))
    def _():
        begin(asw_ref, a_ref, lsw_ref, l_ref, 0)

    @pl.when(live & (core == 1))
    def _():
        begin(a_ref, asw_ref, l_ref, lsw_ref, H)

    @pl.when(live)
    def _():
        bank.wait(0)
        a3 = split(jnp.where(row == 1, 0.0, bank.get(0)))
        bank.wait_half(1)
        out_ref[:, :, :H] = mm(a3, buf[1, :, :H], ta=True).reshape(16, 32, H)
        bank.wait_half(2)
        l2 = split(buf[2, :, :H])
        out_ref[:, :, H:N] = mm(a3, l2, ta=True).reshape(16, 32, H)
        bank.wait(3)
        out_ref[:, :, N:] = mm(bank.get(3), l2, ta=True).reshape(16, 32, H)

    @pl.when(jnp.logical_not(live))
    def _():
        out_ref[...] = jnp.zeros(out_ref.shape, F32)


def k_first(pos_ref, l_ref, lsw_ref, inv_ref, x12_ref, buf, sem):
    row, xl, core = pos_ref[0], pos_ref[1], pos_ref[2]
    bank = Bank(buf, sem)
    live = (xl == 1) & (row <= 1)

    @pl.when(live & (row == core))
    def _():
        bank.start(0, l_ref)
        bank.start(1, lsw_ref)

    @pl.when(live & (row != core))
    def _():
        bank.start(0, lsw_ref)
        bank.start(1, l_ref)

    @pl.when(live)
    def _():
        bank.wait(0)
        inverse_lower(bank.at(0), inv_ref)
        bank.wait(1)
        x12_ref[...] = mm(inv_ref[...], bank.get(1))


def k_second(pos_ref, l_ref, kq_ref, kqsw_ref, first_ref, x12_ref, inv_ref, x_ref, out_ref, buf, sem):
    row, xl, core = pos_ref[0], pos_ref[1], pos_ref[2]
    bank = Bank(buf, sem)
    even = (xl == 0) & (row <= 1)
    odd = (xl == 1) & (row <= 1)

    @pl.when(even & (row == core))
    def _():
        bank.start(0, kq_ref)

    @pl.when(even & (row != core))
    def _():
        bank.start(0, kqsw_ref)

    @pl.when(even)
    def _():
        bank.start(1, l_ref)

    @pl.when(even & (core == 0))
    def _():
        bank.start_half(2, kq_ref, 0)

    @pl.when(even & (core == 1))
    def _():
        bank.start_half(2, kqsw_ref, H)

    @pl.when(odd & (row == 1) & (core == 0))
    def _():
        bank.start(1, x12_ref)

    @pl.when(odd & (row == core))
    def _():
        bank.start(1, first_ref)

    @pl.when(even)
    def _():
        bank.wait(0)
        inverse_lower(bank.at(0), inv_ref)
        bank.wait(1)
        inv = split(inv_ref[...])
        x = mm(inv, bank.get(1))
        x_ref[...] = x
        out_ref[:, :, :N] = x.reshape(16, 32, N)
        bank.wait_half(2)
        half = jnp.where(row == 1, mm(inv, buf[2, :, :H]), 0.0)
        out_ref[:, :, N:] = half.reshape(16, 32, H)

    @pl.when(odd & ((row == 1) | (core == 0)))
    def _():
        bank.wait(1)
        out_ref[:, :, :N] = bank.get(1).reshape(16, 32, N)
        out_ref[:, :, N:] = jnp.zeros((16, 32, H), F32)

    @pl.when((row >= 2) | ((xl == 1) & (row == 0) & (core == 1)))
    def _():
        out_ref[...] = jnp.zeros(out_ref.shape, F32)


def k_send(pos_ref, ac_ref, acsw_ref, l_ref, part_ref, other_ref, out_ref, buf, sem):
    row, xl, core = pos_ref[0], pos_ref[1], pos_ref[2]
    bank = Bank(buf, sem)
    live = (xl == 0) & (row >= 1)

    @pl.when(live & (core == 0))
    def _():
        bank.start(0, acsw_ref)
        bank.start(2, ac_ref)

    @pl.when(live & (core == 1))
    def _():
        bank.start(0, ac_ref)
        bank.start(2, acsw_ref)

    @pl.when(live)
    def _():
        bank.start(1, l_ref)
        bank.wait(0, 1)
        l = split(bank.get(1))
        a3 = jnp.where(row == 1, 0.0, bank.get(0))
        out_ref[:, :, :N] = mm(a3, l, ta=True).reshape(16, 32, N)
        bank.wait(2)
        out_ref[:, :, N:] = mm(bank.get(2), l, ta=True).reshape(16, 32, N)

    @pl.when(xl == 1)
    def _():
        s = part_ref[...] + other_ref[...]
        out_ref[:, :, :N + H] = jnp.broadcast_to(s[None], (16, 32, N + H))
        out_ref[:, :, N + H:] = jnp.zeros((16, 32, H), F32)

    @pl.when((xl == 0) & (row == 0))
    def _():
        out_ref[...] = jnp.zeros(out_ref.shape, F32)


def k_own(got_ref, out_ref, buf, sem):
    total = got_ref[0]
    for s in range(1, 16):
        total = total + got_ref[s]
    out_ref[...] = total


def k_spread(a_ref, b_ref, out_ref, buf, sem):
    s = a_ref[...] + b_ref[...]
    out_ref[...] = jnp.broadcast_to(s[None], out_ref.shape)


def join(bank, slot, core, here, there):
    for c, (left, right) in enumerate(((0, H), (H, 0))):
        @pl.when(core == c)
        def _():
            pltpu.make_async_copy(here, bank.buf.at[slot, :, left:left + H], bank.sem.at[slot]).start()
            pltpu.make_async_copy(there, bank.buf.at[slot, :, right:right + H], bank.sem.at[slot]).start()


def rows_of(bank, slot, src, lo, width):
    for s in range(16):
        pltpu.make_async_copy(
            src.at[s, :, lo:lo + width], bank.buf.at[slot, s * 32:(s + 1) * 32, :width],
            bank.sem.at[slot]).start()


def tril_half(x, core):
    i = lax.broadcasted_iota(jnp.int32, x.shape, 0)
    j = lax.broadcasted_iota(jnp.int32, x.shape, 1) + core * H
    return jnp.where(i >= j, x, 0.0)


def k_one_p(pos_ref, got_ref, a_ref, asw_ref, l_ref, lsw_ref, i1_ref, p_ref, buf, sem):
    row, xl, core = pos_ref[0], pos_ref[1], pos_ref[2]
    bank = Bank(buf, sem)

    @pl.when((xl == 1) & (row == 1))
    def _():
        rows_of(bank, 0, got_ref, 0, H)
        bank.start(1, i1_ref)

        @pl.when(core == 0)
        def _():
            bank.start_half(2, asw_ref, 0)
            bank.start(3, lsw_ref)

        @pl.when(core == 1)
        def _():
            bank.start_half(2, a_ref, H)
            bank.start(3, l_ref)

        bank.wait_half(0)
        bank.wait(1)
        g = mm(bank.get(1), buf[0, :, :H], ta=True)
        bank.wait_half(2)
        g = tril_half(buf[2, :, :H] - g, core)
        bank.wait(3)
        p_ref[...] = mm(tril(bank.get(3)), g, ta=True)


def k_one_w(pos_ref, got_ref, p_ref, psw_ref, a_ref, asw_ref, i1_ref, x12_ref, sym_ref, w_ref, ap_ref, buf, sem):
    row, xl, core = pos_ref[0], pos_ref[1], pos_ref[2]
    bank = Bank(buf, sem)

    @pl.when((xl == 1) & (row == 1))
    def _():
        join(bank, 0, core, p_ref, psw_ref)
        rows_of(bank, 1, got_ref, H, H)
        bank.start(3, i1_ref)

        @pl.when(core == 0)
        def _():
            bank.start_half(2, x12_ref, 0)
            bank.start_half(4, a_ref, 0)

        @pl.when(core == 1)
        def _():
            bank.start_half(2, x12_ref, H)
            bank.start_half(4, asw_ref, H)

        bank.wait(0)
        sym = sym_half(bank.get(0))
        sym_ref[...] = sym
        bank.wait_half(1, 2)
        w = buf[1, :, :H] + 2.0 * mm(sym, buf[2, :, :H])
        w_ref[...] = w
        bank.wait(3)
        bank.wait_half(4)
        ap_ref[...] = buf[4, :, :H] - mm(bank.get(3), w, ta=True)


def k_zero_base(pos_ref, got_ref, t12_ref, t12sw_ref, a_ref, asw_ref, i2_ref, x12_ref, x12sw_ref, base_ref, buf, sem):
    row, xl, core = pos_ref[0], pos_ref[1], pos_ref[2]
    bank = Bank(buf, sem)

    @pl.when((xl == 1) & (row == 0))
    def _():
        for c, (left, right) in enumerate(((t12_ref, t12sw_ref), (t12sw_ref, t12_ref))):
            @pl.when(core == c)
            def _():
                for s in range(16):
                    at = pl.ds(s * 32, 32)
                    pltpu.make_async_copy(left.at[s], buf.at[0, at, :H], sem.at[0]).start()
                    pltpu.make_async_copy(right.at[s], buf.at[0, at, H:], sem.at[0]).start()

        rows_of(bank, 2, got_ref, N, H)
        bank.start(3, i2_ref)

        @pl.when(core == 0)
        def _():
            bank.start_half(1, x12_ref, 0)
            bank.start_half(4, a_ref, 0)

        @pl.when(core == 1)
        def _():
            bank.start_half(1, x12sw_ref, H)
            bank.start_half(4, asw_ref, H)

        bank.wait(0)
        bank.wait_half(1)
        inner = mm(bank.get(0), buf[1, :, :H], ta=True)
        bank.wait_half(2)
        bank.wait(3)
        inner = mm(bank.get(3), buf[2, :, :H] - inner, ta=True)
        bank.wait_half(4)
        base_ref[...] = buf[4, :, :H] - inner


def k_zero_w(pos_ref, got_ref, p_ref, psw_ref, x12_ref, x12sw_ref, w_ref, buf, sem):
    row, xl, core = pos_ref[0], pos_ref[1], pos_ref[2]
    bank = Bank(buf, sem)

    @pl.when((xl == 1) & (row == 0))
    def _():
        join(bank, 0, core, p_ref, psw_ref)
        rows_of(bank, 1, got_ref, H, H)

        @pl.when(core == 0)
        def _():
            bank.start_half(2, x12_ref, 0)

        @pl.when(core == 1)
        def _():
            bank.start_half(2, x12sw_ref, H)

        bank.wait(0)
        sym = sym_half(bank.get(0))
        bank.wait_half(1, 2)
        w_ref[...] = buf[1, :, :H] + 2.0 * mm(sym, buf[2, :, :H])


def k_zero_p(pos_ref, base_ref, w_ref, x12_ref, x12sw_ref, i2_ref, l_ref, lsw_ref, p_ref, buf, sem):
    row, xl, core = pos_ref[0], pos_ref[1], pos_ref[2]
    bank = Bank(buf, sem)

    @pl.when((xl == 1) & (row == 0))
    def _():
        bank.start_half(0, w_ref, 0)

        @pl.when(core == 0)
        def _():
            bank.start(1, x12_ref)
            bank.start(3, l_ref)

        @pl.when(core == 1)
        def _():
            bank.start(1, x12sw_ref)
            bank.start(3, lsw_ref)

        bank.start(2, i2_ref)
        bank.start_half(4, base_ref, 0)
        bank.wait_half(0)
        bank.wait(1)
        inner = mm(bank.get(1), buf[0, :, :H], ta=True)
        bank.wait(2)
        inner = mm(bank.get(2), inner, ta=True)
        bank.wait_half(4)
        g = tril_half(buf[4, :, :H] + inner, core)
        bank.wait(3)
        p_ref[...] = mm(tril(bank.get(3)), g, ta=True)


def k_ends(pos_ref, sym1_ref, p_ref, psw_ref, inv_ref, e_ref, buf, sem):
    row, xl, core = pos_ref[0], pos_ref[1], pos_ref[2]
    bank = Bank(buf, sem)

    @pl.when((xl == 1) & (row == 0) & (core == 0))
    def _():
        join(bank, 0, core, p_ref, psw_ref)
        bank.wait(0)
        buf[0] = sym_half(buf[0])

    @pl.when((xl == 1) & (row == 1) & (core == 1))
    def _():
        bank.start(0, sym1_ref)
        bank.wait(0)

    @pl.when((xl == 1) & (((row == 1) & (core == 1)) | ((row == 0) & (core == 0))))
    def _():
        bank.start(1, inv_ref)
        bank.wait(1)
        inv = split(bank.get(1))
        e_ref[...] = mm(inv, mm(bank.get(0), inv), ta=True)


def even_zero(row, xl, core):
    return (xl == 0) & (row == 0)


def k_before(pos_ref, xs_ref, xh_ref, ts_ref, w_ref, wsw_ref, out_ref, buf, sem):
    row, xl, core = pos_ref[0], pos_ref[1], pos_ref[2]
    bank = Bank(buf, sem)

    @pl.when((xl == 0) & (row == 0))
    def _():
        rows_of(bank, 0, ts_ref, 0, N)
        join(bank, 1, core, xs_ref.at[:, 2 * N:], xh_ref)
        join(bank, 2, core, w_ref, wsw_ref)
        bank.start(3, xs_ref.at[:, N:2 * N])
        rows_of(bank, 4, ts_ref, N, N)
        bank.wait(0, 1)
        inner = mm(bank.get(1), bank.get(0), ta=True)
        bank.wait(2, 3)
        inner = inner + mm(bank.get(2), bank.get(3), ta=True)
        bank.wait(4)
        out_ref[...] = bank.get(4) - inner


def k_final(pos_ref, a_ref, asw_ref, ac_ref, acsw_ref, xs_ref, xh_ref, ts_ref, inv_ref, x_ref, one_ref, onesw_ref, w_ref, wsw_ref, pre_ref, p_ref, psw_ref, ap_ref, apsw_ref, e_ref, res, buf, sem):
    row, xl, core = pos_ref[0], pos_ref[1], pos_ref[2]
    bank = Bank(buf, sem)
    X1, X2, X12, A, A3, A2 = 0, 1, 2, 3, 4, 5
    SYM, W, T, INV, XOWN, L1 = 2, 4, 5, 6, 7, 8

    def x2(slot):
        bank.start(slot, xs_ref.at[:, :N])

    def x1(slot):
        bank.start(slot, xs_ref.at[:, N:2 * N])

    def x12(slot):
        join(bank, slot, core, xs_ref.at[:, 2 * N:], xh_ref)

    low_even = (row >= 2) & (xl == 0)

    @pl.when(low_even)
    def _():
        @pl.when(core == 0)
        def _():
            bank.start(A3, acsw_ref)
            bank.start(A2, ac_ref)

        @pl.when(core == 1)
        def _():
            bank.start(A3, ac_ref)
            bank.start(A2, acsw_ref)

        x12(X12)
        x1(X1)
        x2(X2)
        bank.start(A, a_ref)
        bank.wait(A3, A2, X12)
        a3 = split(bank.get(A3))
        moved = bank.get(A2) - mm(a3, bank.get(X12))
        bank.wait(X1, A)
        res[...] = bank.get(A) - mm(a3, bank.get(X1))
        bank.wait(X2)
        res[...] -= mm(moved, bank.get(X2))

    @pl.when((row >= 2) & (xl == 1) & (core == 0))
    def _():
        bank.start(A3, asw_ref)
        x1(X1)
        bank.start(A, a_ref)
        x2(X2)
        bank.wait(A3, X1, A)
        moved = bank.get(A) - mm(bank.get(A3), bank.get(X1))
        bank.wait(X2)
        res[...] = mm(moved, bank.get(X2))

    @pl.when((row >= 2) & (xl == 1) & (core == 1))
    def _():
        bank.start(A, a_ref)
        x1(X1)
        bank.wait(A, X1)
        res[...] = mm(bank.get(A), bank.get(X1))

    @pl.when((row == 1) & (xl == 0))
    def _():
        bank.start(INV, inv_ref)

        @pl.when(core == 0)
        def _():
            bank.start(L1, ac_ref)

        @pl.when(core == 1)
        def _():
            bank.start(L1, acsw_ref)

        join(bank, W, core, w_ref, wsw_ref)
        x2(X2)
        join(bank, SYM, core, one_ref, onesw_ref)
        bank.start(XOWN, x_ref)
        rows_of(bank, T, ts_ref, 0, N)
        bank.start(A, a_ref)
        bank.wait(INV, L1, W)
        inv = split(bank.get(INV))
        ap = bank.get(L1) - mm(inv, bank.get(W), ta=True)
        bank.wait(X2)
        side = mm(ap, bank.get(X2))
        bank.wait(SYM, XOWN)
        inner = 2.0 * mm(sym_half(bank.get(SYM)), bank.get(XOWN))
        bank.wait(T, A)
        res[...] = bank.get(A) - side - mm(inv, inner + bank.get(T), ta=True)

    @pl.when((row == 0) & (xl == 0))
    def _():
        join(bank, SYM, core, p_ref, psw_ref)
        bank.start(XOWN, x_ref)
        bank.start(T, pre_ref)
        bank.start(INV, inv_ref)
        bank.start(A, a_ref)
        bank.wait(SYM, XOWN)
        inner = 2.0 * mm(sym_half(bank.get(SYM)), bank.get(XOWN))
        bank.wait(T, INV, A)
        res[...] = bank.get(A) - mm(bank.get(INV), inner + bank.get(T), ta=True)

    @pl.when((row == 1) & (xl == 1) & (core == 0))
    def _():
        join(bank, A, core, ap_ref, apsw_ref)
        x2(X2)
        bank.wait(A, X2)
        res[...] = mm(bank.get(A), bank.get(X2))

    def keep(src):
        bank.start(A, src)
        bank.wait(A)
        res[...] = bank.get(A)

    @pl.when((row == 1) & (xl == 1) & (core == 1))
    def _():
        keep(e_ref)

    @pl.when((row == 0) & (xl == 1) & (core == 0))
    def _():
        keep(e_ref)

    @pl.when((row == 0) & (xl == 1) & (core == 1))
    def _():
        keep(a_ref)


def move(x, pairs):
    return lax.ppermute(x, ALL, [(dev(*a), dev(*b)) for a, b in pairs])


def exchange_cores(x, rows, columns):
    return move(x, [((r, c), (r, c ^ 1)) for r in rows for c in columns])


def swap_xh(x):
    return lax.ppermute(x, "xh", [(0, 1), (1, 0)])


def every(x):
    return lax.all_to_all(x, PLANE, 0, 0, tiled=True)


def local(low, adj):
    rows = range(32)
    below = range(2, 32)
    y, xh, z = (lax.axis_index(n) for n in ("y", "xh", "z"))
    xl, core = lax.axis_index("xl"), lax.axis_index("core")
    pos = jnp.stack([y * 8 + xh * 4 + z, xl, core, z]).astype(jnp.int32)
    tile, half = (N, N), (N, H)
    after = lax.optimization_barrier

    adj_sw = exchange_cores(adj, rows, (2, 3))
    low_sw = exchange_cores(low, rows, (2, 3))
    kq = move(low, [((1, 3), (1, 1)), ((0, 2), (0, 0)), ((1, 2), (1, 0))])

    sums_odd, = call(k_sum_odd, [(16, 32, N + H)], pos, adj, adj_sw, low, low_sw, slots=4)
    got = every(sums_odd)
    ac = move(adj, [((r, c), (r, c - 2)) for r in below for c in (2, 3)] + [((1, 2), (1, 0))])

    inv_odd, x12 = call(k_first, [tile, tile], pos, low, low_sw, slots=2, only=odd_top)
    kq, inv_odd = after((kq, inv_odd))
    kq_sw = exchange_cores(kq, (0, 1), (0, 1))
    inv, x, send_x = call(
        k_second, [tile, tile, (16, 32, N + H)], pos, low, kq, kq_sw, inv_odd, x12, slots=3)
    x12_zero = move(x12, [((1, 2), (0, 2))])
    x12_zero_sw = exchange_cores(x12_zero, (0,), (2,))
    got, send_x = after((got, send_x))
    got_x = every(send_x)

    part = jnp.sum(got, axis=0)
    other = swap_xh(part)
    ac, send_x = after((ac, send_x))
    ac_sw = exchange_cores(ac, range(1, 32), (0, 1))
    send, = call(k_send, [(16, 32, 2 * N)], pos, ac, ac_sw, low, part, other, slots=3, near=(4, 5))
    send, got_x = after((send, got_x))
    sums = every(send)
    xs = jnp.concatenate([got_x[0, :, :N], got_x[1]], 1)
    xs = xs + lax.ppermute(xs, "xh", [(0, 1)])
    sums, xs, x12_zero_sw = after((sums, xs, x12_zero_sw))
    xs = lax.all_gather(xs, PLANE, tiled=True)

    p1, = call(k_one_p, [half], pos, sums, adj, adj_sw, low, low_sw, inv_odd, slots=4, only=odd_one)
    p1_zero = move(p1, [((1, c), (0, c)) for c in (2, 3)])
    p1_one = move(p1, [((1, 2), (1, 0)), ((1, 3), (1, 1))])
    p1_sw = exchange_cores(p1, (1,), (2, 3))

    sums_own, p1 = after((sums, p1))
    own, = call(k_own, [(32, 2 * N)], sums_own, near=(0,))
    send, = call(
        k_spread, [(16, 32, 2 * N)], own, lax.ppermute(own, "xh", [(1, 0)]), near=(0, 1))
    ts = every(send)

    t12 = sums[:, :, H:N]
    t12_sw = exchange_cores(t12, (0,), (2, 3))
    base, = call(
        k_zero_base, [half], pos, sums, t12, t12_sw, adj, adj_sw, inv_odd, x12_zero, x12_zero_sw,
        slots=5, only=odd_zero)
    sym1, w1, ap = call(
        k_one_w, [tile, half, half], pos, sums, p1, p1_sw, adj, adj_sw, inv_odd, x12, slots=5, only=odd_one)
    w_one = move(w1, [((1, 2), (1, 0)), ((1, 3), (1, 1))])

    p1_zero, base, send = after((p1_zero, base, send))
    p1_zero_sw = exchange_cores(p1_zero, (0,), (2, 3))
    w0, = call(
        k_zero_w, [half], pos, sums, p1_zero, p1_zero_sw, x12_zero, x12_zero_sw, slots=3, only=odd_zero)
    w_zero = move(w0, [((0, 2), (0, 0)), ((0, 3), (0, 1))])
    p2, = call(
        k_zero_p, [half], pos, base, w0, x12_zero, x12_zero_sw, inv_odd, low, low_sw, slots=5, only=odd_zero)
    p2_zero = move(p2, [((0, 2), (0, 0)), ((0, 3), (0, 1))])
    p2_sw = exchange_cores(p2, (0,), (3,))
    ap_sw = exchange_cores(ap, (1,), (3,))
    e, = call(k_ends, [tile], pos, sym1, p2, p2_sw, inv_odd, slots=2, only=odd_top)

    p1_one_sw = exchange_cores(p1_one, (1,), (0, 1))
    w_one_sw = exchange_cores(w_one, (1,), (0, 1))
    w_zero_sw = exchange_cores(w_zero, (0,), (0, 1))
    xs_sw = exchange_cores(xs[:, 2 * N:], rows, (0, 1))
    pre, = call(
        k_before, [tile], pos, xs, xs_sw, ts, w_zero, w_zero_sw, slots=5, only=even_zero)
    p2_zero_sw = exchange_cores(p2_zero, (0,), (0, 1))
    out, = call(
        k_final, [adj.shape], pos, adj, adj_sw, ac, ac_sw, xs, xs_sw, ts, inv, x,
        p1_one, p1_one_sw, w_one, w_one_sw, pre, p2_zero, p2_zero_sw, ap, ap_sw, e, slots=9)
    return out


def solution(mesh):
    fine = Mesh(mesh.devices.reshape(4, 2, 4, 2, 2), ALL)
    placed = P(None, ("y", "xh", "z"), None, ("xl", "core"))
    return jax.shard_map(
        local, mesh=fine, in_specs=(placed, placed), out_specs=placed, check_vma=False
    )
```

```python
import jax
import jax.numpy as jnp
from jax import lax
from jax.sharding import Mesh
from jax.sharding import PartitionSpec as P
from jax.experimental import pallas as pl
from jax.experimental.pallas import tpu as pltpu

N = 512
H = 256
ALL = ("y", "xh", "z", "xl", "core")
PLANE = ("y", "z")
F32 = jnp.float32
BF16 = jnp.bfloat16


def dev(row, column):
    return row * 4 + column


def split(x):
    hi = x.astype(BF16)
    return hi, (x - hi.astype(F32)).astype(BF16)


def as_parts(x):
    return x if isinstance(x, tuple) else split(x)


def mm(a, b, ta=False):
    ah, al = as_parts(a)
    bh, bl = as_parts(b)
    dims = (((0 if ta else 1,), (0,)), ((), ()))

    def dot(u, v):
        return lax.dot_general(u, v, dims, preferred_element_type=F32)

    return dot(ah, bh) + (dot(ah, bl) + dot(al, bh))


def iotas(n):
    return (
        lax.broadcasted_iota(jnp.int32, (n, n), 0),
        lax.broadcasted_iota(jnp.int32, (n, n), 1),
    )


def tril(x):
    i, j = iotas(x.shape[0])
    return jnp.where(i >= j, x, 0.0)


def sym_half(p):
    i, j = iotas(p.shape[0])
    low = jnp.where(i > j, p, jnp.where(i == j, 0.5 * p, 0.0))
    return 0.5 * (low + low.T)


def inverse_lower(k_ref, out_ref):
    b = 128
    i, j = iotas(b)
    inv, blocks = [], []
    for s in range(4):
        t = k_ref[s * b:(s + 1) * b, s * b:(s + 1) * b]
        on = jnp.where(i == j, t, 0.0)
        down = 1.0 / jnp.sum(on, axis=1, keepdims=True)
        across = 1.0 / jnp.sum(on, axis=0, keepdims=True)
        off = (i // 2 == j // 2) & (i > j)
        inv.append(jnp.where(i == j, down, 0.0) - jnp.where(off, down * t * across, 0.0))
        blocks.append(t)
    size = 2
    while size < b:
        off = (i // (2 * size) == j // (2 * size)) & (i // size > j // size)
        parts = [split(x) for x in inv]
        half = [mm(jnp.where(off, t, 0.0), x) for t, x in zip(blocks, parts)]
        inv = [x - mm(p, h) for x, p, h in zip(inv, parts, half)]
        size *= 2
    out_ref[...] = jnp.zeros((N, N), F32)
    for s in range(4):
        out_ref[s * b:(s + 1) * b, s * b:(s + 1) * b] = inv[s]
    for s in (0, 2):
        low = k_ref[(s + 1) * b:(s + 2) * b, s * b:(s + 1) * b]
        out_ref[(s + 1) * b:(s + 2) * b, s * b:(s + 1) * b] = -mm(inv[s + 1], mm(low, inv[s]))
    top = out_ref[:H, :H]
    bottom = out_ref[H:, H:]
    out_ref[H:, :H] = -mm(bottom, mm(k_ref[H:, :H], top))


class Bank:
    def __init__(self, buf, sem):
        self.buf, self.sem = buf, sem

    def at(self, slot):
        return self.buf.at[slot]

    def start(self, slot, src):
        pltpu.make_async_copy(flat(src), self.buf.at[slot], self.sem.at[slot]).start()

    def start_half(self, slot, src, lo):
        pltpu.make_async_copy(
            flat(src).at[:, lo:lo + H], self.buf.at[slot, :, :H], self.sem.at[slot]).start()

    def wait(self, *slots):
        for s in slots:
            pltpu.make_async_copy(self.buf.at[s], self.buf.at[s], self.sem.at[s]).wait()

    def wait_half(self, *slots):
        for s in slots:
            half = self.buf.at[s, :, :H]
            pltpu.make_async_copy(half, half, self.sem.at[s]).wait()

    def get(self, slot):
        return self.buf[slot]


def flat(ref):
    return ref.at[0, :, 0, :] if len(ref.shape) == 4 else ref


def odd_top(row, xl, core):
    return (xl == 1) & (row <= 1)


def odd_zero(row, xl, core):
    return (xl == 1) & (row == 0)


def odd_one(row, xl, core):
    return (xl == 1) & (row == 1)


LIMIT = 58 * 1024 * 1024


def call(kernel, outs, *args, slots=1, near=(), only=None):
    vm = pl.BlockSpec(memory_space=pltpu.VMEM)
    sm = pl.BlockSpec(memory_space=pltpu.SMEM)
    far = pl.BlockSpec(memory_space=pl.ANY)
    n, m = len(args), len(outs)

    def body(*refs):
        ins, out_refs, built = refs[:n], refs[n:n + m], refs[n + m:n + 2 * m]
        buf, sem, done = refs[n + 2 * m:]
        kernel(*ins, *built, buf, sem)
        copies = [pltpu.make_async_copy(b, flat(o), done.at[i]) for i, (b, o) in enumerate(zip(built, out_refs))]

        def store():
            for c in copies:
                c.start()
            for c in copies:
                c.wait()

        if only is None:
            store()
        else:
            pl.when(only(*(ins[0][i] for i in range(3))))(store)

    return pl.pallas_call(
        body,
        out_shape=[jax.ShapeDtypeStruct(s, F32) for s in outs],
        in_specs=[sm if a.dtype == jnp.int32 else vm if i in near else far for i, a in enumerate(args)],
        out_specs=[far] * m,
        scratch_shapes=[pltpu.VMEM((s[1], s[3]) if len(s) == 4 else s, F32) for s in outs] + [
            pltpu.VMEM((slots, N, N), F32), pltpu.SemaphoreType.DMA((slots,)), pltpu.SemaphoreType.DMA((m,))],
        compiler_params=pltpu.CompilerParams(vmem_limit_bytes=LIMIT),
    )(*args)


def k_sum_odd(pos_ref, a_ref, asw_ref, l_ref, lsw_ref, out_ref, buf, sem):
    row, xl, core = pos_ref[0], pos_ref[1], pos_ref[2]
    bank = Bank(buf, sem)
    live = (row >= 1) & (xl == 1)

    def begin(a3, a2, l3, l2, lo):
        bank.start(0, a3)
        bank.start_half(1, l3, lo)
        bank.start_half(2, l2, lo)
        bank.start(3, a2)

    @pl.when(live & (core == 0))
    def _():
        begin(asw_ref, a_ref, lsw_ref, l_ref, 0)

    @pl.when(live & (core == 1))
    def _():
        begin(a_ref, asw_ref, l_ref, lsw_ref, H)

    @pl.when(live)
    def _():
        bank.wait(0)
        a3 = split(jnp.where(row == 1, 0.0, bank.get(0)))
        bank.wait_half(1)
        out_ref[:, :, :H] = mm(a3, buf[1, :, :H], ta=True).reshape(16, 32, H)
        bank.wait_half(2)
        l2 = split(buf[2, :, :H])
        out_ref[:, :, H:N] = mm(a3, l2, ta=True).reshape(16, 32, H)
        bank.wait(3)
        out_ref[:, :, N:] = mm(bank.get(3), l2, ta=True).reshape(16, 32, H)

    @pl.when(jnp.logical_not(live))
    def _():
        out_ref[...] = jnp.zeros(out_ref.shape, F32)


def k_first(pos_ref, l_ref, lsw_ref, inv_ref, x12_ref, buf, sem):
    row, xl, core = pos_ref[0], pos_ref[1], pos_ref[2]
    bank = Bank(buf, sem)
    live = (xl == 1) & (row <= 1)

    @pl.when(live & (row == core))
    def _():
        bank.start(0, l_ref)
        bank.start(1, lsw_ref)

    @pl.when(live & (row != core))
    def _():
        bank.start(0, lsw_ref)
        bank.start(1, l_ref)

    @pl.when(live)
    def _():
        bank.wait(0)
        inverse_lower(bank.at(0), inv_ref)
        bank.wait(1)
        x12_ref[...] = mm(inv_ref[...], bank.get(1))


def k_second(pos_ref, l_ref, kq_ref, kqsw_ref, first_ref, x12_ref, inv_ref, x_ref, out_ref, buf, sem):
    row, xl, core = pos_ref[0], pos_ref[1], pos_ref[2]
    bank = Bank(buf, sem)
    even = (xl == 0) & (row <= 1)
    odd = (xl == 1) & (row <= 1)

    @pl.when(even & (row == core))
    def _():
        bank.start(0, kq_ref)

    @pl.when(even & (row != core))
    def _():
        bank.start(0, kqsw_ref)

    @pl.when(even)
    def _():
        bank.start(1, l_ref)

    @pl.when(even & (core == 0))
    def _():
        bank.start_half(2, kq_ref, 0)

    @pl.when(even & (core == 1))
    def _():
        bank.start_half(2, kqsw_ref, H)

    @pl.when(odd & (row == 1) & (core == 0))
    def _():
        bank.start(1, x12_ref)

    @pl.when(odd & (row == core))
    def _():
        bank.start(1, first_ref)

    @pl.when(even)
    def _():
        bank.wait(0)
        inverse_lower(bank.at(0), inv_ref)
        bank.wait(1)
        inv = split(inv_ref[...])
        x = mm(inv, bank.get(1))
        x_ref[...] = x
        out_ref[:, :, :N] = x.reshape(16, 32, N)
        bank.wait_half(2)
        half = jnp.where(row == 1, mm(inv, buf[2, :, :H]), 0.0)
        out_ref[:, :, N:] = half.reshape(16, 32, H)

    @pl.when(odd & ((row == 1) | (core == 0)))
    def _():
        bank.wait(1)
        out_ref[:, :, :N] = bank.get(1).reshape(16, 32, N)
        out_ref[:, :, N:] = jnp.zeros((16, 32, H), F32)

    @pl.when((row >= 2) | ((xl == 1) & (row == 0) & (core == 1)))
    def _():
        out_ref[...] = jnp.zeros(out_ref.shape, F32)


def k_send(pos_ref, ac_ref, acsw_ref, l_ref, part_ref, other_ref, out_ref, buf, sem):
    row, xl, core = pos_ref[0], pos_ref[1], pos_ref[2]
    bank = Bank(buf, sem)
    live = (xl == 0) & (row >= 1)

    @pl.when(live & (core == 0))
    def _():
        bank.start(0, acsw_ref)
        bank.start(2, ac_ref)

    @pl.when(live & (core == 1))
    def _():
        bank.start(0, ac_ref)
        bank.start(2, acsw_ref)

    @pl.when(live)
    def _():
        bank.start(1, l_ref)
        bank.wait(0, 1)
        l = split(bank.get(1))
        a3 = jnp.where(row == 1, 0.0, bank.get(0))
        out_ref[:, :, :N] = mm(a3, l, ta=True).reshape(16, 32, N)
        bank.wait(2)
        out_ref[:, :, N:] = mm(bank.get(2), l, ta=True).reshape(16, 32, N)

    @pl.when(xl == 1)
    def _():
        s = part_ref[...] + other_ref[...]
        out_ref[:, :, :N + H] = jnp.broadcast_to(s[None], (16, 32, N + H))
        out_ref[:, :, N + H:] = jnp.zeros((16, 32, H), F32)

    @pl.when((xl == 0) & (row == 0))
    def _():
        out_ref[...] = jnp.zeros(out_ref.shape, F32)


def k_own(got_ref, out_ref, buf, sem):
    total = got_ref[0]
    for s in range(1, 16):
        total = total + got_ref[s]
    out_ref[...] = total


def k_spread(a_ref, b_ref, out_ref, buf, sem):
    s = a_ref[...] + b_ref[...]
    out_ref[...] = jnp.broadcast_to(s[None], out_ref.shape)


def join(bank, slot, core, here, there):
    for c, (left, right) in enumerate(((0, H), (H, 0))):
        @pl.when(core == c)
        def _():
            pltpu.make_async_copy(here, bank.buf.at[slot, :, left:left + H], bank.sem.at[slot]).start()
            pltpu.make_async_copy(there, bank.buf.at[slot, :, right:right + H], bank.sem.at[slot]).start()


def rows_of(bank, slot, src, lo, width):
    for s in range(16):
        pltpu.make_async_copy(
            src.at[s, :, lo:lo + width], bank.buf.at[slot, s * 32:(s + 1) * 32, :width],
            bank.sem.at[slot]).start()


def tril_half(x, core):
    i = lax.broadcasted_iota(jnp.int32, x.shape, 0)
    j = lax.broadcasted_iota(jnp.int32, x.shape, 1) + core * H
    return jnp.where(i >= j, x, 0.0)


def k_one_p(pos_ref, got_ref, a_ref, asw_ref, l_ref, lsw_ref, i1_ref, p_ref, buf, sem):
    row, xl, core = pos_ref[0], pos_ref[1], pos_ref[2]
    bank = Bank(buf, sem)

    @pl.when((xl == 1) & (row == 1))
    def _():
        rows_of(bank, 0, got_ref, 0, H)
        bank.start(1, i1_ref)

        @pl.when(core == 0)
        def _():
            bank.start_half(2, asw_ref, 0)
            bank.start(3, lsw_ref)

        @pl.when(core == 1)
        def _():
            bank.start_half(2, a_ref, H)
            bank.start(3, l_ref)

        bank.wait_half(0)
        bank.wait(1)
        g = mm(bank.get(1), buf[0, :, :H], ta=True)
        bank.wait_half(2)
        g = tril_half(buf[2, :, :H] - g, core)
        bank.wait(3)
        p_ref[...] = mm(tril(bank.get(3)), g, ta=True)


def k_one_w(pos_ref, got_ref, p_ref, psw_ref, a_ref, asw_ref, i1_ref, x12_ref, w_ref, ap_ref, buf, sem):
    row, xl, core = pos_ref[0], pos_ref[1], pos_ref[2]
    bank = Bank(buf, sem)

    @pl.when((xl == 1) & (row == 1))
    def _():
        join(bank, 0, core, p_ref, psw_ref)
        rows_of(bank, 1, got_ref, H, H)
        bank.start(3, i1_ref)

        @pl.when(core == 0)
        def _():
            bank.start_half(2, x12_ref, 0)
            bank.start_half(4, a_ref, 0)

        @pl.when(core == 1)
        def _():
            bank.start_half(2, x12_ref, H)
            bank.start_half(4, asw_ref, H)

        bank.wait(0)
        sym = sym_half(bank.get(0))
        bank.wait_half(1, 2)
        w = buf[1, :, :H] + 2.0 * mm(sym, buf[2, :, :H])
        w_ref[...] = w
        bank.wait(3)
        bank.wait_half(4)
        ap_ref[...] = buf[4, :, :H] - mm(bank.get(3), w, ta=True)


def k_zero_base(pos_ref, got_ref, t12_ref, t12sw_ref, a_ref, asw_ref, i2_ref, x12_ref, x12sw_ref, base_ref, buf, sem):
    row, xl, core = pos_ref[0], pos_ref[1], pos_ref[2]
    bank = Bank(buf, sem)

    @pl.when((xl == 1) & (row == 0))
    def _():
        for c, (left, right) in enumerate(((t12_ref, t12sw_ref), (t12sw_ref, t12_ref))):
            @pl.when(core == c)
            def _():
                for s in range(16):
                    at = pl.ds(s * 32, 32)
                    pltpu.make_async_copy(left.at[s], buf.at[0, at, :H], sem.at[0]).start()
                    pltpu.make_async_copy(right.at[s], buf.at[0, at, H:], sem.at[0]).start()

        rows_of(bank, 2, got_ref, N, H)
        bank.start(3, i2_ref)

        @pl.when(core == 0)
        def _():
            bank.start_half(1, x12_ref, 0)
            bank.start_half(4, a_ref, 0)

        @pl.when(core == 1)
        def _():
            bank.start_half(1, x12sw_ref, H)
            bank.start_half(4, asw_ref, H)

        bank.wait(0)
        bank.wait_half(1)
        inner = mm(bank.get(0), buf[1, :, :H], ta=True)
        bank.wait_half(2)
        bank.wait(3)
        inner = mm(bank.get(3), buf[2, :, :H] - inner, ta=True)
        bank.wait_half(4)
        base_ref[...] = buf[4, :, :H] - inner


def k_zero_w(pos_ref, got_ref, p_ref, psw_ref, x12_ref, x12sw_ref, w_ref, buf, sem):
    row, xl, core = pos_ref[0], pos_ref[1], pos_ref[2]
    bank = Bank(buf, sem)

    @pl.when((xl == 1) & (row == 0))
    def _():
        join(bank, 0, core, p_ref, psw_ref)
        rows_of(bank, 1, got_ref, H, H)

        @pl.when(core == 0)
        def _():
            bank.start_half(2, x12_ref, 0)

        @pl.when(core == 1)
        def _():
            bank.start_half(2, x12sw_ref, H)

        bank.wait(0)
        sym = sym_half(bank.get(0))
        bank.wait_half(1, 2)
        w_ref[...] = buf[1, :, :H] + 2.0 * mm(sym, buf[2, :, :H])


def k_zero_p(pos_ref, base_ref, w_ref, x12_ref, x12sw_ref, i2_ref, l_ref, lsw_ref, p_ref, buf, sem):
    row, xl, core = pos_ref[0], pos_ref[1], pos_ref[2]
    bank = Bank(buf, sem)

    @pl.when((xl == 1) & (row == 0))
    def _():
        bank.start_half(0, w_ref, 0)

        @pl.when(core == 0)
        def _():
            bank.start(1, x12_ref)
            bank.start(3, l_ref)

        @pl.when(core == 1)
        def _():
            bank.start(1, x12sw_ref)
            bank.start(3, lsw_ref)

        bank.start(2, i2_ref)
        bank.start_half(4, base_ref, 0)
        bank.wait_half(0)
        bank.wait(1)
        inner = mm(bank.get(1), buf[0, :, :H], ta=True)
        bank.wait(2)
        inner = mm(bank.get(2), inner, ta=True)
        bank.wait_half(4)
        g = tril_half(buf[4, :, :H] + inner, core)
        bank.wait(3)
        p_ref[...] = mm(tril(bank.get(3)), g, ta=True)


def k_final(pos_ref, a_ref, asw_ref, ac_ref, acsw_ref, xs_ref, xh_ref, ts_ref, inv_ref, x_ref, one_ref, onesw_ref, w_ref, wsw_ref, wz_ref, wzsw_ref, p_ref, psw_ref, ap_ref, apsw_ref, p1_ref, p1sw_ref, p2_ref, p2sw_ref, invo_ref, res, buf, sem):
    row, xl, core = pos_ref[0], pos_ref[1], pos_ref[2]
    bank = Bank(buf, sem)
    X1, X2, X12, A, A3, A2 = 0, 1, 2, 3, 4, 5
    SYM, W, T, INV, XOWN, L1 = 2, 4, 5, 6, 7, 8

    def x2(slot):
        bank.start(slot, xs_ref.at[:, :N])

    def x1(slot):
        bank.start(slot, xs_ref.at[:, N:2 * N])

    def x12(slot):
        join(bank, slot, core, xs_ref.at[:, 2 * N:], xh_ref)

    low_even = (row >= 2) & (xl == 0)

    @pl.when(low_even)
    def _():
        @pl.when(core == 0)
        def _():
            bank.start(A3, acsw_ref)
            bank.start(A2, ac_ref)

        @pl.when(core == 1)
        def _():
            bank.start(A3, ac_ref)
            bank.start(A2, acsw_ref)

        x12(X12)
        x1(X1)
        x2(X2)
        bank.start(A, a_ref)
        bank.wait(A3, A2, X12)
        a3 = split(bank.get(A3))
        moved = bank.get(A2) - mm(a3, bank.get(X12))
        bank.wait(X1, A)
        res[...] = bank.get(A) - mm(a3, bank.get(X1))
        bank.wait(X2)
        res[...] -= mm(moved, bank.get(X2))

    @pl.when((row >= 2) & (xl == 1) & (core == 0))
    def _():
        bank.start(A3, asw_ref)
        x1(X1)
        bank.start(A, a_ref)
        x2(X2)
        bank.wait(A3, X1, A)
        moved = bank.get(A) - mm(bank.get(A3), bank.get(X1))
        bank.wait(X2)
        res[...] = mm(moved, bank.get(X2))

    @pl.when((row >= 2) & (xl == 1) & (core == 1))
    def _():
        bank.start(A, a_ref)
        x1(X1)
        bank.wait(A, X1)
        res[...] = mm(bank.get(A), bank.get(X1))

    @pl.when((row == 1) & (xl == 0))
    def _():
        bank.start(INV, inv_ref)

        @pl.when(core == 0)
        def _():
            bank.start(L1, ac_ref)

        @pl.when(core == 1)
        def _():
            bank.start(L1, acsw_ref)

        join(bank, W, core, w_ref, wsw_ref)
        x2(X2)
        join(bank, SYM, core, one_ref, onesw_ref)
        bank.start(XOWN, x_ref)
        rows_of(bank, T, ts_ref, 0, N)
        bank.start(A, a_ref)
        bank.wait(INV, L1, W)
        inv = split(bank.get(INV))
        ap = bank.get(L1) - mm(inv, bank.get(W), ta=True)
        bank.wait(X2)
        side = mm(ap, bank.get(X2))
        bank.wait(SYM, XOWN)
        inner = 2.0 * mm(sym_half(bank.get(SYM)), bank.get(XOWN))
        bank.wait(T, A)
        res[...] = bank.get(A) - side - mm(inv, inner + bank.get(T), ta=True)

    @pl.when((row == 0) & (xl == 0))
    def _():
        x12(X12)
        rows_of(bank, T, ts_ref, 0, N)
        join(bank, W, core, wz_ref, wzsw_ref)
        x1(X1)
        rows_of(bank, X2, ts_ref, N, N)
        join(bank, L1, core, p_ref, psw_ref)
        bank.start(XOWN, x_ref)
        bank.start(INV, inv_ref)
        bank.start(A, a_ref)
        bank.wait(X12, T)
        inner = mm(bank.get(X12), bank.get(T), ta=True)
        bank.wait(W, X1)
        inner = inner + mm(bank.get(W), bank.get(X1), ta=True)
        bank.wait(L1, XOWN, X2)
        inner = bank.get(X2) - inner + 2.0 * mm(sym_half(bank.get(L1)), bank.get(XOWN))
        bank.wait(INV, A)
        res[...] = bank.get(A) - mm(bank.get(INV), inner, ta=True)

    @pl.when((row == 1) & (xl == 1) & (core == 0))
    def _():
        join(bank, A, core, ap_ref, apsw_ref)
        x2(X2)
        bank.wait(A, X2)
        res[...] = mm(bank.get(A), bank.get(X2))

    def end(here, there):
        join(bank, SYM, core, here, there)
        bank.start(INV, invo_ref)
        bank.wait(SYM, INV)
        inv = split(bank.get(INV))
        res[...] = mm(inv, mm(sym_half(bank.get(SYM)), inv), ta=True)

    @pl.when((row == 1) & (xl == 1) & (core == 1))
    def _():
        end(p1_ref, p1sw_ref)

    @pl.when((row == 0) & (xl == 1) & (core == 0))
    def _():
        end(p2_ref, p2sw_ref)

    @pl.when((row == 0) & (xl == 1) & (core == 1))
    def _():
        bank.start(A, a_ref)
        bank.wait(A)
        res[...] = bank.get(A)


def move(x, pairs):
    return lax.ppermute(x, ALL, [(dev(*a), dev(*b)) for a, b in pairs])


def exchange_cores(x, rows, columns):
    return move(x, [((r, c), (r, c ^ 1)) for r in rows for c in columns])


def swap_xh(x):
    return lax.ppermute(x, "xh", [(0, 1), (1, 0)])


def every(x):
    return lax.all_to_all(x, PLANE, 0, 0, tiled=True)


def local(low, adj):
    rows = range(32)
    below = range(2, 32)
    y, xh, z = (lax.axis_index(n) for n in ("y", "xh", "z"))
    xl, core = lax.axis_index("xl"), lax.axis_index("core")
    pos = jnp.stack([y * 8 + xh * 4 + z, xl, core, z]).astype(jnp.int32)
    tile, half = (N, N), (N, H)
    after = lax.optimization_barrier

    adj_sw = exchange_cores(adj, rows, (2, 3))
    low_sw = exchange_cores(low, rows, (2, 3))
    kq = move(low, [((1, 3), (1, 1)), ((0, 2), (0, 0)), ((1, 2), (1, 0))])

    sums_odd, = call(k_sum_odd, [(16, 32, N + H)], pos, adj, adj_sw, low, low_sw, slots=4)
    got = every(sums_odd)
    ac = move(adj, [((r, c), (r, c - 2)) for r in below for c in (2, 3)] + [((1, 2), (1, 0))])

    inv_odd, x12 = call(k_first, [tile, tile], pos, low, low_sw, slots=2, only=odd_top)
    kq, inv_odd = after((kq, inv_odd))
    kq_sw = exchange_cores(kq, (0, 1), (0, 1))
    inv, x, send_x = call(
        k_second, [tile, tile, (16, 32, N + H)], pos, low, kq, kq_sw, inv_odd, x12, slots=3)
    x12_zero = move(x12, [((1, 2), (0, 2))])
    x12_zero_sw = exchange_cores(x12_zero, (0,), (2,))
    got, send_x = after((got, send_x))
    got_x = every(send_x)

    part = jnp.sum(got, axis=0)
    other = swap_xh(part)
    ac, send_x = after((ac, send_x))
    ac_sw = exchange_cores(ac, range(1, 32), (0, 1))
    send, = call(k_send, [(16, 32, 2 * N)], pos, ac, ac_sw, low, part, other, slots=3, near=(4, 5))
    send, got_x = after((send, got_x))
    sums = every(send)
    xs = jnp.concatenate([got_x[0, :, :N], got_x[1]], 1)
    xs = xs + lax.ppermute(xs, "xh", [(0, 1)])
    sums, xs, x12_zero_sw = after((sums, xs, x12_zero_sw))
    xs = lax.all_gather(xs, PLANE, tiled=True)

    p1, = call(k_one_p, [half], pos, sums, adj, adj_sw, low, low_sw, inv_odd, slots=4, only=odd_one)
    p1_zero = move(p1, [((1, c), (0, c)) for c in (2, 3)])
    p1_one = move(p1, [((1, 2), (1, 0)), ((1, 3), (1, 1))])
    p1_sw = exchange_cores(p1, (1,), (2, 3))

    sums_own, p1 = after((sums, p1))
    own, = call(k_own, [(32, 2 * N)], sums_own, near=(0,))
    send, = call(
        k_spread, [(16, 32, 2 * N)], own, lax.ppermute(own, "xh", [(1, 0)]), near=(0, 1))
    ts = every(send)

    t12 = sums[:, :, H:N]
    t12_sw = exchange_cores(t12, (0,), (2, 3))
    base, = call(
        k_zero_base, [half], pos, sums, t12, t12_sw, adj, adj_sw, inv_odd, x12_zero, x12_zero_sw,
        slots=5, only=odd_zero)
    w1, ap = call(
        k_one_w, [half, half], pos, sums, p1, p1_sw, adj, adj_sw, inv_odd, x12, slots=5, only=odd_one)
    w_one = move(w1, [((1, 2), (1, 0)), ((1, 3), (1, 1))])

    p1_zero, base, send = after((p1_zero, base, send))
    p1_zero_sw = exchange_cores(p1_zero, (0,), (2, 3))
    w0, = call(
        k_zero_w, [half], pos, sums, p1_zero, p1_zero_sw, x12_zero, x12_zero_sw, slots=3, only=odd_zero)
    w_zero = move(w0, [((0, 2), (0, 0)), ((0, 3), (0, 1))])
    p2, = call(
        k_zero_p, [half], pos, base, w0, x12_zero, x12_zero_sw, inv_odd, low, low_sw, slots=5, only=odd_zero)
    p2_zero = move(p2, [((0, 2), (0, 0)), ((0, 3), (0, 1))])
    p2_sw = exchange_cores(p2, (0,), (3,))
    ap_sw = exchange_cores(ap, (1,), (3,))

    p1_one_sw = exchange_cores(p1_one, (1,), (0, 1))
    w_one_sw = exchange_cores(w_one, (1,), (0, 1))
    w_zero_sw = exchange_cores(w_zero, (0,), (0, 1))
    xs, p1_one_sw, w_zero_sw, ap_sw = after((xs, p1_one_sw, w_zero_sw, ap_sw))
    xs_sw = exchange_cores(xs[:, 2 * N:], rows, (0, 1))
    p2_zero_sw = exchange_cores(p2_zero, (0,), (0, 1))
    out, = call(
        k_final, [adj.shape], pos, adj, adj_sw, ac, ac_sw, xs, xs_sw, ts, inv, x,
        p1_one, p1_one_sw, w_one, w_one_sw, w_zero, w_zero_sw, p2_zero, p2_zero_sw, ap, ap_sw,
        p1, p1_sw, p2, p2_sw, inv_odd, slots=9)
    return out


def solution(mesh):
    fine = Mesh(mesh.devices.reshape(4, 2, 4, 2, 2), ALL)
    placed = P(None, ("y", "xh", "z"), None, ("xl", "core"))
    return jax.shard_map(
        local, mesh=fine, in_specs=(placed, placed), out_specs=placed, check_vma=False
    )
```

```python
import jax
import jax.numpy as jnp
from jax import lax
from jax.sharding import Mesh
from jax.sharding import PartitionSpec as P
from jax.experimental import pallas as pl
from jax.experimental.pallas import tpu as pltpu

N = 512
H = 256
ALL = ("y", "xh", "z", "xl", "core")
PLANE = ("y", "z")
F32 = jnp.float32
BF16 = jnp.bfloat16


def dev(row, column):
    return row * 4 + column


def split(x):
    hi = x.astype(BF16)
    return hi, (x - hi.astype(F32)).astype(BF16)


def as_parts(x):
    return x if isinstance(x, tuple) else split(x)


def mm(a, b, ta=False):
    ah, al = as_parts(a)
    bh, bl = as_parts(b)
    dims = (((0 if ta else 1,), (0,)), ((), ()))

    def dot(u, v):
        return lax.dot_general(u, v, dims, preferred_element_type=F32)

    return dot(ah, bh) + (dot(ah, bl) + dot(al, bh))


def iotas(n):
    return (
        lax.broadcasted_iota(jnp.int32, (n, n), 0),
        lax.broadcasted_iota(jnp.int32, (n, n), 1),
    )


def tril(x):
    i, j = iotas(x.shape[0])
    return jnp.where(i >= j, x, 0.0)


def sym_half(p):
    i, j = iotas(p.shape[0])
    low = jnp.where(i > j, p, jnp.where(i == j, 0.5 * p, 0.0))
    return 0.5 * (low + low.T)


def inverse_lower(k_ref, out_ref):
    b = 128
    i, j = iotas(b)
    inv, blocks = [], []
    for s in range(4):
        t = k_ref[s * b:(s + 1) * b, s * b:(s + 1) * b]
        on = jnp.where(i == j, t, 0.0)
        down = 1.0 / jnp.sum(on, axis=1, keepdims=True)
        across = 1.0 / jnp.sum(on, axis=0, keepdims=True)
        off = (i // 2 == j // 2) & (i > j)
        inv.append(jnp.where(i == j, down, 0.0) - jnp.where(off, down * t * across, 0.0))
        blocks.append(t)
    size = 2
    while size < b:
        off = (i // (2 * size) == j // (2 * size)) & (i // size > j // size)
        parts = [split(x) for x in inv]
        half = [mm(jnp.where(off, t, 0.0), x) for t, x in zip(blocks, parts)]
        inv = [x - mm(p, h) for x, p, h in zip(inv, parts, half)]
        size *= 2
    out_ref[...] = jnp.zeros((N, N), F32)
    for s in range(4):
        out_ref[s * b:(s + 1) * b, s * b:(s + 1) * b] = inv[s]
    for s in (0, 2):
        low = k_ref[(s + 1) * b:(s + 2) * b, s * b:(s + 1) * b]
        out_ref[(s + 1) * b:(s + 2) * b, s * b:(s + 1) * b] = -mm(inv[s + 1], mm(low, inv[s]))
    top = out_ref[:H, :H]
    bottom = out_ref[H:, H:]
    out_ref[H:, :H] = -mm(bottom, mm(k_ref[H:, :H], top))


class Bank:
    def __init__(self, buf, sem):
        self.buf, self.sem = buf, sem

    def at(self, slot):
        return self.buf.at[slot]

    def start(self, slot, src):
        pltpu.make_async_copy(flat(src), self.buf.at[slot], self.sem.at[slot]).start()

    def start_half(self, slot, src, lo):
        pltpu.make_async_copy(
            flat(src).at[:, lo:lo + H], self.buf.at[slot, :, :H], self.sem.at[slot]).start()

    def wait(self, *slots):
        for s in slots:
            pltpu.make_async_copy(self.buf.at[s], self.buf.at[s], self.sem.at[s]).wait()

    def wait_half(self, *slots):
        for s in slots:
            half = self.buf.at[s, :, :H]
            pltpu.make_async_copy(half, half, self.sem.at[s]).wait()

    def get(self, slot):
        return self.buf[slot]


def flat(ref):
    return ref.at[0, :, 0, :] if len(ref.shape) == 4 else ref


def odd_top(row, xl, core):
    return (xl == 1) & (row <= 1)


def odd_zero(row, xl, core):
    return (xl == 1) & (row == 0)


def odd_one(row, xl, core):
    return (xl == 1) & (row == 1)


LIMIT = 58 * 1024 * 1024


def call(kernel, outs, *args, slots=1, near=(), only=None):
    vm = pl.BlockSpec(memory_space=pltpu.VMEM)
    sm = pl.BlockSpec(memory_space=pltpu.SMEM)
    far = pl.BlockSpec(memory_space=pl.ANY)
    n, m = len(args), len(outs)

    def body(*refs):
        ins, out_refs, built = refs[:n], refs[n:n + m], refs[n + m:n + 2 * m]
        buf, sem, done = refs[n + 2 * m:]
        kernel(*ins, *built, buf, sem)
        copies = [pltpu.make_async_copy(b, flat(o), done.at[i]) for i, (b, o) in enumerate(zip(built, out_refs))]

        def store():
            for c in copies:
                c.start()
            for c in copies:
                c.wait()

        if only is None:
            store()
        else:
            pl.when(only(*(ins[0][i] for i in range(3))))(store)

    return pl.pallas_call(
        body,
        out_shape=[jax.ShapeDtypeStruct(s, F32) for s in outs],
        in_specs=[sm if a.dtype == jnp.int32 else vm if i in near else far for i, a in enumerate(args)],
        out_specs=[far] * m,
        scratch_shapes=[pltpu.VMEM((s[1], s[3]) if len(s) == 4 else s, F32) for s in outs] + [
            pltpu.VMEM((slots, N, N), F32), pltpu.SemaphoreType.DMA((slots,)), pltpu.SemaphoreType.DMA((m,))],
        compiler_params=pltpu.CompilerParams(vmem_limit_bytes=LIMIT),
    )(*args)


def k_sum_odd(pos_ref, a_ref, asw_ref, l_ref, lsw_ref, out_ref, buf, sem):
    row, xl, core = pos_ref[0], pos_ref[1], pos_ref[2]
    bank = Bank(buf, sem)
    live = (row >= 1) & (xl == 1)

    def begin(a3, a2, l3, l2, lo):
        bank.start(0, a3)
        bank.start_half(1, l3, lo)
        bank.start_half(2, l2, lo)
        bank.start(3, a2)

    @pl.when(live & (core == 0))
    def _():
        begin(asw_ref, a_ref, lsw_ref, l_ref, 0)

    @pl.when(live & (core == 1))
    def _():
        begin(a_ref, asw_ref, l_ref, lsw_ref, H)

    @pl.when(live)
    def _():
        bank.wait(0)
        a3 = split(jnp.where(row == 1, 0.0, bank.get(0)))
        bank.wait_half(1)
        out_ref[:, :, :H] = mm(a3, buf[1, :, :H], ta=True).reshape(16, 32, H)
        bank.wait_half(2)
        l2 = split(buf[2, :, :H])
        out_ref[:, :, H:N] = mm(a3, l2, ta=True).reshape(16, 32, H)
        bank.wait(3)
        out_ref[:, :, N:] = mm(bank.get(3), l2, ta=True).reshape(16, 32, H)

    @pl.when(jnp.logical_not(live))
    def _():
        out_ref[...] = jnp.zeros(out_ref.shape, F32)


def k_first(pos_ref, l_ref, lsw_ref, inv_ref, x12_ref, buf, sem):
    row, xl, core = pos_ref[0], pos_ref[1], pos_ref[2]
    bank = Bank(buf, sem)
    live = (xl == 1) & (row <= 1)

    @pl.when(live & (row == core))
    def _():
        bank.start(0, l_ref)
        bank.start(1, lsw_ref)

    @pl.when(live & (row != core))
    def _():
        bank.start(0, lsw_ref)
        bank.start(1, l_ref)

    @pl.when(live)
    def _():
        bank.wait(0)
        inverse_lower(bank.at(0), inv_ref)
        bank.wait(1)
        x12_ref[...] = mm(inv_ref[...], bank.get(1))


def k_second(pos_ref, l_ref, kq_ref, kqsw_ref, first_ref, x12_ref, inv_ref, x_ref, out_ref, buf, sem):
    row, xl, core = pos_ref[0], pos_ref[1], pos_ref[2]
    bank = Bank(buf, sem)
    even = (xl == 0) & (row <= 1)
    odd = (xl == 1) & (row <= 1)

    @pl.when(even & (row == core))
    def _():
        bank.start(0, kq_ref)

    @pl.when(even & (row != core))
    def _():
        bank.start(0, kqsw_ref)

    @pl.when(even)
    def _():
        bank.start(1, l_ref)

    @pl.when(even & (core == 0))
    def _():
        bank.start_half(2, kq_ref, 0)

    @pl.when(even & (core == 1))
    def _():
        bank.start_half(2, kqsw_ref, H)

    @pl.when(odd & (row == 1) & (core == 0))
    def _():
        bank.start(1, x12_ref)

    @pl.when(odd & (row == core))
    def _():
        bank.start(1, first_ref)

    @pl.when(even)
    def _():
        bank.wait(0)
        inverse_lower(bank.at(0), inv_ref)
        bank.wait(1)
        inv = split(inv_ref[...])
        x = mm(inv, bank.get(1))
        x_ref[...] = x
        out_ref[:, :, :N] = x.reshape(16, 32, N)
        bank.wait_half(2)
        half = jnp.where(row == 1, mm(inv, buf[2, :, :H]), 0.0)
        out_ref[:, :, N:] = half.reshape(16, 32, H)

    @pl.when(odd & ((row == 1) | (core == 0)))
    def _():
        bank.wait(1)
        out_ref[:, :, :N] = bank.get(1).reshape(16, 32, N)
        out_ref[:, :, N:] = jnp.zeros((16, 32, H), F32)

    @pl.when((row >= 2) | ((xl == 1) & (row == 0) & (core == 1)))
    def _():
        out_ref[...] = jnp.zeros(out_ref.shape, F32)


def k_send(pos_ref, ac_ref, acsw_ref, l_ref, part_ref, other_ref, out_ref, buf, sem):
    row, xl, core = pos_ref[0], pos_ref[1], pos_ref[2]
    bank = Bank(buf, sem)
    live = (xl == 0) & (row >= 1)

    @pl.when(live & (core == 0))
    def _():
        bank.start(0, acsw_ref)
        bank.start(2, ac_ref)

    @pl.when(live & (core == 1))
    def _():
        bank.start(0, ac_ref)
        bank.start(2, acsw_ref)

    @pl.when(live)
    def _():
        bank.start(1, l_ref)
        bank.wait(0, 1)
        l = split(bank.get(1))
        a3 = jnp.where(row == 1, 0.0, bank.get(0))
        out_ref[:, :, :N] = mm(a3, l, ta=True).reshape(16, 32, N)
        bank.wait(2)
        out_ref[:, :, N:] = mm(bank.get(2), l, ta=True).reshape(16, 32, N)

    @pl.when(xl == 1)
    def _():
        s = part_ref[...] + other_ref[...]
        out_ref[:, :, :N + H] = jnp.broadcast_to(s[None], (16, 32, N + H))
        out_ref[:, :, N + H:] = jnp.zeros((16, 32, H), F32)

    @pl.when((xl == 0) & (row == 0))
    def _():
        out_ref[...] = jnp.zeros(out_ref.shape, F32)


def k_own(got_ref, out_ref, buf, sem):
    total = got_ref[0]
    for s in range(1, 16):
        total = total + got_ref[s]
    out_ref[...] = total


def k_spread(a_ref, b_ref, out_ref, buf, sem):
    s = a_ref[...] + b_ref[...]
    out_ref[...] = jnp.broadcast_to(s[None], out_ref.shape)


def join(bank, slot, core, here, there):
    for c, (left, right) in enumerate(((0, H), (H, 0))):
        @pl.when(core == c)
        def _():
            pltpu.make_async_copy(here, bank.buf.at[slot, :, left:left + H], bank.sem.at[slot]).start()
            pltpu.make_async_copy(there, bank.buf.at[slot, :, right:right + H], bank.sem.at[slot]).start()


def join_slices(bank, slot, core, here, there):
    for c, (left, right) in enumerate(((here, there), (there, here))):
        @pl.when(core == c)
        def _():
            for s in range(16):
                at = pl.ds(s * 32, 32)
                pltpu.make_async_copy(left.at[s], bank.buf.at[slot, at, :H], bank.sem.at[slot]).start()
                pltpu.make_async_copy(right.at[s], bank.buf.at[slot, at, H:], bank.sem.at[slot]).start()


def rows_of(bank, slot, src, lo, width):
    for s in range(16):
        pltpu.make_async_copy(
            src.at[s, :, lo:lo + width], bank.buf.at[slot, s * 32:(s + 1) * 32, :width],
            bank.sem.at[slot]).start()


def tril_half(x, core):
    i = lax.broadcasted_iota(jnp.int32, x.shape, 0)
    j = lax.broadcasted_iota(jnp.int32, x.shape, 1) + core * H
    return jnp.where(i >= j, x, 0.0)


def k_one_p(pos_ref, got_ref, a_ref, asw_ref, l_ref, lsw_ref, i1_ref, p_ref, buf, sem):
    row, xl, core = pos_ref[0], pos_ref[1], pos_ref[2]
    bank = Bank(buf, sem)

    @pl.when((xl == 1) & (row == 1))
    def _():
        rows_of(bank, 0, got_ref, 0, H)
        bank.start(1, i1_ref)

        @pl.when(core == 0)
        def _():
            bank.start_half(2, asw_ref, 0)
            bank.start(3, lsw_ref)

        @pl.when(core == 1)
        def _():
            bank.start_half(2, a_ref, H)
            bank.start(3, l_ref)

        bank.wait_half(0)
        bank.wait(1)
        g = mm(bank.get(1), buf[0, :, :H], ta=True)
        bank.wait_half(2)
        g = tril_half(buf[2, :, :H] - g, core)
        bank.wait(3)
        p_ref[...] = mm(tril(bank.get(3)), g, ta=True)


def k_one_w(pos_ref, got_ref, p_ref, psw_ref, a_ref, asw_ref, i1_ref, x12_ref, w_ref, ap_ref, buf, sem):
    row, xl, core = pos_ref[0], pos_ref[1], pos_ref[2]
    bank = Bank(buf, sem)

    @pl.when((xl == 1) & (row == 1))
    def _():
        join(bank, 0, core, p_ref, psw_ref)
        rows_of(bank, 1, got_ref, H, H)
        bank.start(3, i1_ref)

        @pl.when(core == 0)
        def _():
            bank.start_half(2, x12_ref, 0)
            bank.start_half(4, a_ref, 0)

        @pl.when(core == 1)
        def _():
            bank.start_half(2, x12_ref, H)
            bank.start_half(4, asw_ref, H)

        bank.wait(0)
        sym = sym_half(bank.get(0))
        bank.wait_half(1, 2)
        w = buf[1, :, :H] + 2.0 * mm(sym, buf[2, :, :H])
        w_ref[...] = w
        bank.wait(3)
        bank.wait_half(4)
        ap_ref[...] = buf[4, :, :H] - mm(bank.get(3), w, ta=True)


def k_zero_base(pos_ref, got_ref, t12_ref, t12sw_ref, a_ref, asw_ref, i2_ref, x12_ref, x12sw_ref, base_ref, buf, sem):
    row, xl, core = pos_ref[0], pos_ref[1], pos_ref[2]
    bank = Bank(buf, sem)

    @pl.when((xl == 1) & (row == 0))
    def _():
        for c, (left, right) in enumerate(((t12_ref, t12sw_ref), (t12sw_ref, t12_ref))):
            @pl.when(core == c)
            def _():
                for s in range(16):
                    at = pl.ds(s * 32, 32)
                    pltpu.make_async_copy(left.at[s], buf.at[0, at, :H], sem.at[0]).start()
                    pltpu.make_async_copy(right.at[s], buf.at[0, at, H:], sem.at[0]).start()

        rows_of(bank, 2, got_ref, N, H)
        bank.start(3, i2_ref)

        @pl.when(core == 0)
        def _():
            bank.start_half(1, x12_ref, 0)
            bank.start_half(4, a_ref, 0)

        @pl.when(core == 1)
        def _():
            bank.start_half(1, x12sw_ref, H)
            bank.start_half(4, asw_ref, H)

        bank.wait(0)
        bank.wait_half(1)
        inner = mm(bank.get(0), buf[1, :, :H], ta=True)
        bank.wait_half(2)
        bank.wait(3)
        inner = mm(bank.get(3), buf[2, :, :H] - inner, ta=True)
        bank.wait_half(4)
        base_ref[...] = buf[4, :, :H] - inner


def k_zero_w(pos_ref, got_ref, p_ref, psw_ref, x12_ref, x12sw_ref, w_ref, buf, sem):
    row, xl, core = pos_ref[0], pos_ref[1], pos_ref[2]
    bank = Bank(buf, sem)

    @pl.when((xl == 1) & (row == 0))
    def _():
        join(bank, 0, core, p_ref, psw_ref)
        rows_of(bank, 1, got_ref, H, H)

        @pl.when(core == 0)
        def _():
            bank.start_half(2, x12_ref, 0)

        @pl.when(core == 1)
        def _():
            bank.start_half(2, x12sw_ref, H)

        bank.wait(0)
        sym = sym_half(bank.get(0))
        bank.wait_half(1, 2)
        w_ref[...] = buf[1, :, :H] + 2.0 * mm(sym, buf[2, :, :H])


def k_zero_p(pos_ref, base_ref, w_ref, x12_ref, x12sw_ref, i2_ref, l_ref, lsw_ref, p_ref, buf, sem):
    row, xl, core = pos_ref[0], pos_ref[1], pos_ref[2]
    bank = Bank(buf, sem)

    @pl.when((xl == 1) & (row == 0))
    def _():
        bank.start_half(0, w_ref, 0)

        @pl.when(core == 0)
        def _():
            bank.start(1, x12_ref)
            bank.start(3, l_ref)

        @pl.when(core == 1)
        def _():
            bank.start(1, x12sw_ref)
            bank.start(3, lsw_ref)

        bank.start(2, i2_ref)
        bank.start_half(4, base_ref, 0)
        bank.wait_half(0)
        bank.wait(1)
        inner = mm(bank.get(1), buf[0, :, :H], ta=True)
        bank.wait(2)
        inner = mm(bank.get(2), inner, ta=True)
        bank.wait_half(4)
        g = tril_half(buf[4, :, :H] + inner, core)
        bank.wait(3)
        p_ref[...] = mm(tril(bank.get(3)), g, ta=True)


def k_final(pos_ref, a_ref, asw_ref, ac_ref, acsw_ref, xs_ref, xh_ref, ts_ref, inv_ref, x_ref, one_ref, onesw_ref, w_ref, wsw_ref, wz_ref, wzsw_ref, p_ref, psw_ref, ap_ref, apsw_ref, p1_ref, p1sw_ref, p2_ref, p2sw_ref, invo_ref, res, buf, sem):
    row, xl, core = pos_ref[0], pos_ref[1], pos_ref[2]
    bank = Bank(buf, sem)
    X1, X2, X12, A, A3, A2 = 0, 1, 2, 3, 4, 5
    SYM, W, T, INV, XOWN, L1 = 2, 4, 5, 6, 7, 8

    def x2(slot):
        rows_of(bank, slot, xs_ref, 0, N)

    def x1(slot):
        rows_of(bank, slot, xs_ref, N, N)

    def x12(slot):
        join_slices(bank, slot, core, xs_ref.at[:, :, 2 * N:], xh_ref)

    low_even = (row >= 2) & (xl == 0)

    @pl.when(low_even)
    def _():
        @pl.when(core == 0)
        def _():
            bank.start(A3, acsw_ref)
            bank.start(A2, ac_ref)

        @pl.when(core == 1)
        def _():
            bank.start(A3, ac_ref)
            bank.start(A2, acsw_ref)

        x12(X12)
        x1(X1)
        x2(X2)
        bank.start(A, a_ref)
        bank.wait(A3, A2, X12)
        a3 = split(bank.get(A3))
        moved = bank.get(A2) - mm(a3, bank.get(X12))
        bank.wait(X1, A)
        res[...] = bank.get(A) - mm(a3, bank.get(X1))
        bank.wait(X2)
        res[...] -= mm(moved, bank.get(X2))

    @pl.when((row >= 2) & (xl == 1) & (core == 0))
    def _():
        bank.start(A3, asw_ref)
        x1(X1)
        bank.start(A, a_ref)
        x2(X2)
        bank.wait(A3, X1, A)
        moved = bank.get(A) - mm(bank.get(A3), bank.get(X1))
        bank.wait(X2)
        res[...] = mm(moved, bank.get(X2))

    @pl.when((row >= 2) & (xl == 1) & (core == 1))
    def _():
        bank.start(A, a_ref)
        x1(X1)
        bank.wait(A, X1)
        res[...] = mm(bank.get(A), bank.get(X1))

    @pl.when((row == 1) & (xl == 0))
    def _():
        bank.start(INV, inv_ref)

        @pl.when(core == 0)
        def _():
            bank.start(L1, ac_ref)

        @pl.when(core == 1)
        def _():
            bank.start(L1, acsw_ref)

        join(bank, W, core, w_ref, wsw_ref)
        x2(X2)
        join(bank, SYM, core, one_ref, onesw_ref)
        bank.start(XOWN, x_ref)
        rows_of(bank, T, ts_ref, 0, N)
        bank.start(A, a_ref)
        bank.wait(INV, L1, W)
        inv = split(bank.get(INV))
        ap = bank.get(L1) - mm(inv, bank.get(W), ta=True)
        bank.wait(X2)
        side = mm(ap, bank.get(X2))
        bank.wait(SYM, XOWN)
        inner = 2.0 * mm(sym_half(bank.get(SYM)), bank.get(XOWN))
        bank.wait(T, A)
        res[...] = bank.get(A) - side - mm(inv, inner + bank.get(T), ta=True)

    @pl.when((row == 0) & (xl == 0))
    def _():
        x12(X12)
        rows_of(bank, T, ts_ref, 0, N)
        join(bank, W, core, wz_ref, wzsw_ref)
        x1(X1)
        rows_of(bank, X2, ts_ref, N, N)
        join(bank, L1, core, p_ref, psw_ref)
        bank.start(XOWN, x_ref)
        bank.start(INV, inv_ref)
        bank.start(A, a_ref)
        bank.wait(X12, T)
        inner = mm(bank.get(X12), bank.get(T), ta=True)
        bank.wait(W, X1)
        inner = inner + mm(bank.get(W), bank.get(X1), ta=True)
        bank.wait(L1, XOWN, X2)
        inner = bank.get(X2) - inner + 2.0 * mm(sym_half(bank.get(L1)), bank.get(XOWN))
        bank.wait(INV, A)
        res[...] = bank.get(A) - mm(bank.get(INV), inner, ta=True)

    @pl.when((row == 1) & (xl == 1) & (core == 0))
    def _():
        join(bank, A, core, ap_ref, apsw_ref)
        x2(X2)
        bank.wait(A, X2)
        res[...] = mm(bank.get(A), bank.get(X2))

    def end(here, there):
        join(bank, SYM, core, here, there)
        bank.start(INV, invo_ref)
        bank.wait(SYM, INV)
        inv = split(bank.get(INV))
        res[...] = mm(inv, mm(sym_half(bank.get(SYM)), inv), ta=True)

    @pl.when((row == 1) & (xl == 1) & (core == 1))
    def _():
        end(p1_ref, p1sw_ref)

    @pl.when((row == 0) & (xl == 1) & (core == 0))
    def _():
        end(p2_ref, p2sw_ref)

    @pl.when((row == 0) & (xl == 1) & (core == 1))
    def _():
        bank.start(A, a_ref)
        bank.wait(A)
        res[...] = bank.get(A)


def move(x, pairs):
    return lax.ppermute(x, ALL, [(dev(*a), dev(*b)) for a, b in pairs])


def exchange_cores(x, rows, columns):
    return move(x, [((r, c), (r, c ^ 1)) for r in rows for c in columns])


def swap_xh(x):
    return lax.ppermute(x, "xh", [(0, 1), (1, 0)])


def every(x):
    return lax.all_to_all(x, PLANE, 0, 0, tiled=True)


def local(low, adj):
    rows = range(32)
    below = range(2, 32)
    y, xh, z = (lax.axis_index(n) for n in ("y", "xh", "z"))
    xl, core = lax.axis_index("xl"), lax.axis_index("core")
    pos = jnp.stack([y * 8 + xh * 4 + z, xl, core, z]).astype(jnp.int32)
    tile, half = (N, N), (N, H)
    after = lax.optimization_barrier

    adj_sw = exchange_cores(adj, rows, (2, 3))
    low_sw = exchange_cores(low, rows, (2, 3))
    kq = move(low, [((1, 3), (1, 1)), ((0, 2), (0, 0)), ((1, 2), (1, 0))])

    sums_odd, = call(k_sum_odd, [(16, 32, N + H)], pos, adj, adj_sw, low, low_sw, slots=4)
    got = every(sums_odd)
    ac = move(adj, [((r, c), (r, c - 2)) for r in below for c in (2, 3)] + [((1, 2), (1, 0))])

    inv_odd, x12 = call(k_first, [tile, tile], pos, low, low_sw, slots=2, only=odd_top)
    kq, inv_odd = after((kq, inv_odd))
    kq_sw = exchange_cores(kq, (0, 1), (0, 1))
    inv, x, send_x = call(
        k_second, [tile, tile, (16, 32, N + H)], pos, low, kq, kq_sw, inv_odd, x12, slots=3)
    x12_zero = move(x12, [((1, 2), (0, 2))])
    x12_zero_sw = exchange_cores(x12_zero, (0,), (2,))
    got, send_x = after((got, send_x))
    got_x = every(send_x)

    part = jnp.sum(got, axis=0)
    other = swap_xh(part)
    ac, send_x = after((ac, send_x))
    ac_sw = exchange_cores(ac, range(1, 32), (0, 1))
    send, = call(k_send, [(16, 32, 2 * N)], pos, ac, ac_sw, low, part, other, slots=3, near=(4, 5))
    send, got_x = after((send, got_x))
    sums = every(send)
    xs = jnp.concatenate([got_x[0, :, :N], got_x[1]], 1)
    spread, = call(
        k_spread, [(16, 32, 2 * N + H)], xs, lax.ppermute(xs, "xh", [(0, 1)]), near=(0, 1))
    sums, spread, x12_zero_sw = after((sums, spread, x12_zero_sw))
    xs = every(spread)

    p1, = call(k_one_p, [half], pos, sums, adj, adj_sw, low, low_sw, inv_odd, slots=4, only=odd_one)
    p1_zero = move(p1, [((1, c), (0, c)) for c in (2, 3)])
    p1_one = move(p1, [((1, 2), (1, 0)), ((1, 3), (1, 1))])
    p1_sw = exchange_cores(p1, (1,), (2, 3))

    sums_own, p1 = after((sums, p1))
    own, = call(k_own, [(32, 2 * N)], sums_own, near=(0,))
    send, = call(
        k_spread, [(16, 32, 2 * N)], own, lax.ppermute(own, "xh", [(1, 0)]), near=(0, 1))
    ts = every(send)

    t12 = sums[:, :, H:N]
    t12_sw = exchange_cores(t12, (0,), (2, 3))
    base, = call(
        k_zero_base, [half], pos, sums, t12, t12_sw, adj, adj_sw, inv_odd, x12_zero, x12_zero_sw,
        slots=5, only=odd_zero)
    w1, ap = call(
        k_one_w, [half, half], pos, sums, p1, p1_sw, adj, adj_sw, inv_odd, x12, slots=5, only=odd_one)
    w_one = move(w1, [((1, 2), (1, 0)), ((1, 3), (1, 1))])

    p1_zero, base, send = after((p1_zero, base, send))
    p1_zero_sw = exchange_cores(p1_zero, (0,), (2, 3))
    w0, = call(
        k_zero_w, [half], pos, sums, p1_zero, p1_zero_sw, x12_zero, x12_zero_sw, slots=3, only=odd_zero)
    w_zero = move(w0, [((0, 2), (0, 0)), ((0, 3), (0, 1))])
    p2, = call(
        k_zero_p, [half], pos, base, w0, x12_zero, x12_zero_sw, inv_odd, low, low_sw, slots=5, only=odd_zero)
    p2_zero = move(p2, [((0, 2), (0, 0)), ((0, 3), (0, 1))])
    p2_sw = exchange_cores(p2, (0,), (3,))
    ap_sw = exchange_cores(ap, (1,), (3,))

    p1_one_sw = exchange_cores(p1_one, (1,), (0, 1))
    w_one_sw = exchange_cores(w_one, (1,), (0, 1))
    xs_sw = exchange_cores(xs[:, :, 2 * N:], rows, (0, 1))
    w_zero, xs_sw, p1_one_sw = after((w_zero, xs_sw, p1_one_sw))
    w_zero_sw = exchange_cores(w_zero, (0,), (0, 1))
    p2_zero, w_zero_sw = after((p2_zero, w_zero_sw))
    p2_zero_sw = exchange_cores(p2_zero, (0,), (0, 1))
    out, = call(
        k_final, [adj.shape], pos, adj, adj_sw, ac, ac_sw, xs, xs_sw, ts, inv, x,
        p1_one, p1_one_sw, w_one, w_one_sw, w_zero, w_zero_sw, p2_zero, p2_zero_sw, ap, ap_sw,
        p1, p1_sw, p2, p2_sw, inv_odd, slots=9)
    return out


def solution(mesh):
    fine = Mesh(mesh.devices.reshape(4, 2, 4, 2, 2), ALL)
    placed = P(None, ("y", "xh", "z"), None, ("xl", "core"))
    return jax.shard_map(
        local, mesh=fine, in_specs=(placed, placed), out_specs=placed, check_vma=False
    )
```

```python
import jax
import jax.numpy as jnp
from jax import lax
from jax.sharding import Mesh
from jax.sharding import PartitionSpec as P
from jax.experimental import pallas as pl
from jax.experimental.pallas import tpu as pltpu

N = 512
H = 256
ALL = ("y", "xh", "z", "xl", "core")
PLANE = ("y", "z")
F32 = jnp.float32
BF16 = jnp.bfloat16


def dev(row, column):
    return row * 4 + column


def split(x):
    hi = x.astype(BF16)
    return hi, (x - hi.astype(F32)).astype(BF16)


def as_parts(x):
    return x if isinstance(x, tuple) else split(x)


def mm(a, b, ta=False):
    ah, al = as_parts(a)
    bh, bl = as_parts(b)
    dims = (((0 if ta else 1,), (0,)), ((), ()))

    def dot(u, v):
        return lax.dot_general(u, v, dims, preferred_element_type=F32)

    return dot(ah, bh) + (dot(ah, bl) + dot(al, bh))


def iotas(n):
    return (
        lax.broadcasted_iota(jnp.int32, (n, n), 0),
        lax.broadcasted_iota(jnp.int32, (n, n), 1),
    )


def tril(x):
    i, j = iotas(x.shape[0])
    return jnp.where(i >= j, x, 0.0)


def sym_half(p):
    i, j = iotas(p.shape[0])
    low = jnp.where(i > j, p, jnp.where(i == j, 0.5 * p, 0.0))
    return 0.5 * (low + low.T)


def inverse_lower(k_ref, out_ref):
    b = 128
    i, j = iotas(b)
    inv, blocks = [], []
    for s in range(4):
        t = k_ref[s * b:(s + 1) * b, s * b:(s + 1) * b]
        on = jnp.where(i == j, t, 0.0)
        down = 1.0 / jnp.sum(on, axis=1, keepdims=True)
        across = 1.0 / jnp.sum(on, axis=0, keepdims=True)
        off = (i // 2 == j // 2) & (i > j)
        inv.append(jnp.where(i == j, down, 0.0) - jnp.where(off, down * t * across, 0.0))
        blocks.append(t)
    size = 2
    while size < b:
        off = (i // (2 * size) == j // (2 * size)) & (i // size > j // size)
        parts = [split(x) for x in inv]
        half = [mm(jnp.where(off, t, 0.0), x) for t, x in zip(blocks, parts)]
        inv = [x - mm(p, h) for x, p, h in zip(inv, parts, half)]
        size *= 2
    out_ref[...] = jnp.zeros((N, N), F32)
    for s in range(4):
        out_ref[s * b:(s + 1) * b, s * b:(s + 1) * b] = inv[s]
    for s in (0, 2):
        low = k_ref[(s + 1) * b:(s + 2) * b, s * b:(s + 1) * b]
        out_ref[(s + 1) * b:(s + 2) * b, s * b:(s + 1) * b] = -mm(inv[s + 1], mm(low, inv[s]))
    top = out_ref[:H, :H]
    bottom = out_ref[H:, H:]
    out_ref[H:, :H] = -mm(bottom, mm(k_ref[H:, :H], top))


class Bank:
    def __init__(self, buf, sem):
        self.buf, self.sem = buf, sem

    def at(self, slot):
        return self.buf.at[slot]

    def start(self, slot, src):
        pltpu.make_async_copy(flat(src), self.buf.at[slot], self.sem.at[slot]).start()

    def start_half(self, slot, src, lo):
        pltpu.make_async_copy(
            flat(src).at[:, lo:lo + H], self.buf.at[slot, :, :H], self.sem.at[slot]).start()

    def wait(self, *slots):
        for s in slots:
            pltpu.make_async_copy(self.buf.at[s], self.buf.at[s], self.sem.at[s]).wait()

    def wait_half(self, *slots):
        for s in slots:
            half = self.buf.at[s, :, :H]
            pltpu.make_async_copy(half, half, self.sem.at[s]).wait()

    def get(self, slot):
        return self.buf[slot]


def flat(ref):
    return ref.at[0, :, 0, :] if len(ref.shape) == 4 else ref


def odd_top(row, xl, core):
    return (xl == 1) & (row <= 1)


def odd_zero(row, xl, core):
    return (xl == 1) & (row == 0)


def odd_one(row, xl, core):
    return (xl == 1) & (row == 1)


LIMIT = 61 * 1024 * 1024


def call(kernel, outs, *args, slots=1, near=(), only=None):
    vm = pl.BlockSpec(memory_space=pltpu.VMEM)
    sm = pl.BlockSpec(memory_space=pltpu.SMEM)
    far = pl.BlockSpec(memory_space=pl.ANY)
    n, m = len(args), len(outs)

    def body(*refs):
        ins, out_refs, built = refs[:n], refs[n:n + m], refs[n + m:n + 2 * m]
        buf, sem, done = refs[n + 2 * m:]
        kernel(*ins, *built, buf, sem)
        copies = [pltpu.make_async_copy(b, flat(o), done.at[i]) for i, (b, o) in enumerate(zip(built, out_refs))]

        def store():
            for c in copies:
                c.start()
            for c in copies:
                c.wait()

        if only is None:
            store()
        else:
            pl.when(only(*(ins[0][i] for i in range(3))))(store)

    return pl.pallas_call(
        body,
        out_shape=[jax.ShapeDtypeStruct(s, F32) for s in outs],
        in_specs=[sm if a.dtype == jnp.int32 else vm if i in near else far for i, a in enumerate(args)],
        out_specs=[far] * m,
        scratch_shapes=[pltpu.VMEM((s[1], s[3]) if len(s) == 4 else s, F32) for s in outs] + [
            pltpu.VMEM((slots, N, N), F32), pltpu.SemaphoreType.DMA((slots,)), pltpu.SemaphoreType.DMA((m,))],
        compiler_params=pltpu.CompilerParams(vmem_limit_bytes=LIMIT),
    )(*args)


def k_sum_odd(pos_ref, a_ref, asw_ref, l_ref, lsw_ref, out_ref, buf, sem):
    row, xl, core = pos_ref[0], pos_ref[1], pos_ref[2]
    bank = Bank(buf, sem)
    live = (row >= 1) & (xl == 1)

    def begin(a3, a2, l3, l2, lo):
        bank.start(0, a3)
        bank.start_half(1, l3, lo)
        bank.start_half(2, l2, lo)
        bank.start(3, a2)

    @pl.when(live & (core == 0))
    def _():
        begin(asw_ref, a_ref, lsw_ref, l_ref, 0)

    @pl.when(live & (core == 1))
    def _():
        begin(a_ref, asw_ref, l_ref, lsw_ref, H)

    @pl.when(live)
    def _():
        bank.wait(0)
        a3 = split(jnp.where(row == 1, 0.0, bank.get(0)))
        bank.wait_half(1)
        out_ref[:, :, :H] = mm(a3, buf[1, :, :H], ta=True).reshape(16, 32, H)
        bank.wait_half(2)
        l2 = split(buf[2, :, :H])
        out_ref[:, :, H:N] = mm(a3, l2, ta=True).reshape(16, 32, H)
        bank.wait(3)
        out_ref[:, :, N:] = mm(bank.get(3), l2, ta=True).reshape(16, 32, H)

    @pl.when(jnp.logical_not(live))
    def _():
        out_ref[...] = jnp.zeros(out_ref.shape, F32)


def k_first(pos_ref, l_ref, lsw_ref, inv_ref, x12_ref, buf, sem):
    row, xl, core = pos_ref[0], pos_ref[1], pos_ref[2]
    bank = Bank(buf, sem)
    live = (xl == 1) & (row <= 1)

    @pl.when(live & (row == core))
    def _():
        bank.start(0, l_ref)
        bank.start(1, lsw_ref)

    @pl.when(live & (row != core))
    def _():
        bank.start(0, lsw_ref)
        bank.start(1, l_ref)

    @pl.when(live)
    def _():
        bank.wait(0)
        inverse_lower(bank.at(0), inv_ref)
        bank.wait(1)
        x12_ref[...] = mm(inv_ref[...], bank.get(1))


def k_second(pos_ref, l_ref, kq_ref, kqsw_ref, first_ref, x12_ref, inv_ref, x_ref, out_ref, buf, sem):
    row, xl, core = pos_ref[0], pos_ref[1], pos_ref[2]
    bank = Bank(buf, sem)
    even = (xl == 0) & (row <= 1)
    odd = (xl == 1) & (row <= 1)

    @pl.when(even & (row == core))
    def _():
        bank.start(0, kq_ref)

    @pl.when(even & (row != core))
    def _():
        bank.start(0, kqsw_ref)

    @pl.when(even)
    def _():
        bank.start(1, l_ref)

    @pl.when(even & (core == 0))
    def _():
        bank.start_half(2, kq_ref, 0)

    @pl.when(even & (core == 1))
    def _():
        bank.start_half(2, kqsw_ref, H)

    @pl.when(odd & (row == 1) & (core == 0))
    def _():
        bank.start(1, x12_ref)

    @pl.when(odd & (row == core))
    def _():
        bank.start(1, first_ref)

    @pl.when(even)
    def _():
        bank.wait(0)
        inverse_lower(bank.at(0), inv_ref)
        bank.wait(1)
        inv = split(inv_ref[...])
        x = mm(inv, bank.get(1))
        x_ref[...] = x
        out_ref[:, :, :N] = x.reshape(16, 32, N)
        bank.wait_half(2)
        half = jnp.where(row == 1, mm(inv, buf[2, :, :H]), 0.0)
        out_ref[:, :, N:] = half.reshape(16, 32, H)

    @pl.when(odd & ((row == 1) | (core == 0)))
    def _():
        bank.wait(1)
        out_ref[:, :, :N] = bank.get(1).reshape(16, 32, N)
        out_ref[:, :, N:] = jnp.zeros((16, 32, H), F32)

    @pl.when((row >= 2) | ((xl == 1) & (row == 0) & (core == 1)))
    def _():
        out_ref[...] = jnp.zeros(out_ref.shape, F32)


def k_send(pos_ref, ac_ref, acsw_ref, l_ref, part_ref, other_ref, out_ref, buf, sem):
    row, xl, core = pos_ref[0], pos_ref[1], pos_ref[2]
    bank = Bank(buf, sem)
    live = (xl == 0) & (row >= 1)

    @pl.when(live & (core == 0))
    def _():
        bank.start(0, acsw_ref)
        bank.start(2, ac_ref)

    @pl.when(live & (core == 1))
    def _():
        bank.start(0, ac_ref)
        bank.start(2, acsw_ref)

    @pl.when(live)
    def _():
        bank.start(1, l_ref)
        bank.wait(0, 1)
        l = split(bank.get(1))
        a3 = jnp.where(row == 1, 0.0, bank.get(0))
        out_ref[:, :, :N] = mm(a3, l, ta=True).reshape(16, 32, N)
        bank.wait(2)
        out_ref[:, :, N:] = mm(bank.get(2), l, ta=True).reshape(16, 32, N)

    @pl.when(xl == 1)
    def _():
        s = part_ref[...] + other_ref[...]
        out_ref[:, :, :N + H] = jnp.broadcast_to(s[None], (16, 32, N + H))
        out_ref[:, :, N + H:] = jnp.zeros((16, 32, H), F32)

    @pl.when((xl == 0) & (row == 0))
    def _():
        out_ref[...] = jnp.zeros(out_ref.shape, F32)


def k_own(got_ref, out_ref, buf, sem):
    total = got_ref[0]
    for s in range(1, 16):
        total = total + got_ref[s]
    out_ref[...] = total


def k_spread(a_ref, b_ref, out_ref, buf, sem):
    s = a_ref[...] + b_ref[...]
    out_ref[...] = jnp.broadcast_to(s[None], out_ref.shape)


def join(bank, slot, core, here, there):
    for c, (left, right) in enumerate(((0, H), (H, 0))):
        @pl.when(core == c)
        def _():
            pltpu.make_async_copy(here, bank.buf.at[slot, :, left:left + H], bank.sem.at[slot]).start()
            pltpu.make_async_copy(there, bank.buf.at[slot, :, right:right + H], bank.sem.at[slot]).start()


def join_slices(bank, slot, core, here, there):
    for c, (left, right) in enumerate(((here, there), (there, here))):
        @pl.when(core == c)
        def _():
            for s in range(16):
                at = pl.ds(s * 32, 32)
                pltpu.make_async_copy(left.at[s], bank.buf.at[slot, at, :H], bank.sem.at[slot]).start()
                pltpu.make_async_copy(right.at[s], bank.buf.at[slot, at, H:], bank.sem.at[slot]).start()


def rows_of(bank, slot, src, lo, width):
    for s in range(16):
        pltpu.make_async_copy(
            src.at[s, :, lo:lo + width], bank.buf.at[slot, s * 32:(s + 1) * 32, :width],
            bank.sem.at[slot]).start()


def tril_half(x, core):
    i = lax.broadcasted_iota(jnp.int32, x.shape, 0)
    j = lax.broadcasted_iota(jnp.int32, x.shape, 1) + core * H
    return jnp.where(i >= j, x, 0.0)


def k_one_p(pos_ref, got_ref, a_ref, asw_ref, l_ref, lsw_ref, i1_ref, p_ref, buf, sem):
    row, xl, core = pos_ref[0], pos_ref[1], pos_ref[2]
    bank = Bank(buf, sem)

    @pl.when((xl == 1) & (row == 1))
    def _():
        rows_of(bank, 0, got_ref, 0, H)
        bank.start(1, i1_ref)

        @pl.when(core == 0)
        def _():
            bank.start_half(2, asw_ref, 0)
            bank.start(3, lsw_ref)

        @pl.when(core == 1)
        def _():
            bank.start_half(2, a_ref, H)
            bank.start(3, l_ref)

        bank.wait_half(0)
        bank.wait(1)
        g = mm(bank.get(1), buf[0, :, :H], ta=True)
        bank.wait_half(2)
        g = tril_half(buf[2, :, :H] - g, core)
        bank.wait(3)
        p_ref[...] = mm(tril(bank.get(3)), g, ta=True)


def k_one_w(pos_ref, got_ref, p_ref, psw_ref, a_ref, asw_ref, i1_ref, x12_ref, w_ref, ap_ref, buf, sem):
    row, xl, core = pos_ref[0], pos_ref[1], pos_ref[2]
    bank = Bank(buf, sem)

    @pl.when((xl == 1) & (row == 1))
    def _():
        join(bank, 0, core, p_ref, psw_ref)
        rows_of(bank, 1, got_ref, H, H)
        bank.start(3, i1_ref)

        @pl.when(core == 0)
        def _():
            bank.start_half(2, x12_ref, 0)
            bank.start_half(4, a_ref, 0)

        @pl.when(core == 1)
        def _():
            bank.start_half(2, x12_ref, H)
            bank.start_half(4, asw_ref, H)

        bank.wait(0)
        sym = sym_half(bank.get(0))
        bank.wait_half(1, 2)
        w = buf[1, :, :H] + 2.0 * mm(sym, buf[2, :, :H])
        w_ref[...] = w
        bank.wait(3)
        bank.wait_half(4)
        ap_ref[...] = buf[4, :, :H] - mm(bank.get(3), w, ta=True)


def k_zero_base(pos_ref, got_ref, t12_ref, t12sw_ref, a_ref, asw_ref, i2_ref, x12_ref, x12sw_ref, base_ref, buf, sem):
    row, xl, core = pos_ref[0], pos_ref[1], pos_ref[2]
    bank = Bank(buf, sem)

    @pl.when((xl == 1) & (row == 0))
    def _():
        for c, (left, right) in enumerate(((t12_ref, t12sw_ref), (t12sw_ref, t12_ref))):
            @pl.when(core == c)
            def _():
                for s in range(16):
                    at = pl.ds(s * 32, 32)
                    pltpu.make_async_copy(left.at[s], buf.at[0, at, :H], sem.at[0]).start()
                    pltpu.make_async_copy(right.at[s], buf.at[0, at, H:], sem.at[0]).start()

        rows_of(bank, 2, got_ref, N, H)
        bank.start(3, i2_ref)

        @pl.when(core == 0)
        def _():
            bank.start_half(1, x12_ref, 0)
            bank.start_half(4, a_ref, 0)

        @pl.when(core == 1)
        def _():
            bank.start_half(1, x12sw_ref, H)
            bank.start_half(4, asw_ref, H)

        bank.wait(0)
        bank.wait_half(1)
        inner = mm(bank.get(0), buf[1, :, :H], ta=True)
        bank.wait_half(2)
        bank.wait(3)
        inner = mm(bank.get(3), buf[2, :, :H] - inner, ta=True)
        bank.wait_half(4)
        base_ref[...] = buf[4, :, :H] - inner


def k_zero_w(pos_ref, got_ref, p_ref, psw_ref, x12_ref, x12sw_ref, w_ref, buf, sem):
    row, xl, core = pos_ref[0], pos_ref[1], pos_ref[2]
    bank = Bank(buf, sem)

    @pl.when((xl == 1) & (row == 0))
    def _():
        join(bank, 0, core, p_ref, psw_ref)
        rows_of(bank, 1, got_ref, H, H)

        @pl.when(core == 0)
        def _():
            bank.start_half(2, x12_ref, 0)

        @pl.when(core == 1)
        def _():
            bank.start_half(2, x12sw_ref, H)

        bank.wait(0)
        sym = sym_half(bank.get(0))
        bank.wait_half(1, 2)
        w_ref[...] = buf[1, :, :H] + 2.0 * mm(sym, buf[2, :, :H])


def k_zero_p(pos_ref, base_ref, w_ref, x12_ref, x12sw_ref, i2_ref, l_ref, lsw_ref, p_ref, buf, sem):
    row, xl, core = pos_ref[0], pos_ref[1], pos_ref[2]
    bank = Bank(buf, sem)

    @pl.when((xl == 1) & (row == 0))
    def _():
        bank.start_half(0, w_ref, 0)

        @pl.when(core == 0)
        def _():
            bank.start(1, x12_ref)
            bank.start(3, l_ref)

        @pl.when(core == 1)
        def _():
            bank.start(1, x12sw_ref)
            bank.start(3, lsw_ref)

        bank.start(2, i2_ref)
        bank.start_half(4, base_ref, 0)
        bank.wait_half(0)
        bank.wait(1)
        inner = mm(bank.get(1), buf[0, :, :H], ta=True)
        bank.wait(2)
        inner = mm(bank.get(2), inner, ta=True)
        bank.wait_half(4)
        g = tril_half(buf[4, :, :H] + inner, core)
        bank.wait(3)
        p_ref[...] = mm(tril(bank.get(3)), g, ta=True)


def k_final(pos_ref, a_ref, asw_ref, ac_ref, acsw_ref, xs_ref, xh_ref, ts_ref, inv_ref, x_ref, one_ref, onesw_ref, w_ref, wsw_ref, wz_ref, wzsw_ref, p_ref, psw_ref, ap_ref, apsw_ref, p1_ref, p1sw_ref, p2_ref, p2sw_ref, invo_ref, res, buf, sem):
    row, xl, core = pos_ref[0], pos_ref[1], pos_ref[2]
    bank = Bank(buf, sem)
    X1, X2, X12, A, A3, A2 = 0, 1, 2, 3, 4, 5
    SYM, W, T, INV, XOWN, L1 = 2, 4, 5, 6, 7, 8

    def x2(slot):
        rows_of(bank, slot, xs_ref, 0, N)

    def x1(slot):
        rows_of(bank, slot, xs_ref, N, N)

    def x12(slot):
        join_slices(bank, slot, core, xs_ref.at[:, :, 2 * N:], xh_ref)

    low_even = (row >= 2) & (xl == 0)

    @pl.when(low_even)
    def _():
        @pl.when(core == 0)
        def _():
            bank.start(A3, acsw_ref)
            bank.start(A2, ac_ref)

        @pl.when(core == 1)
        def _():
            bank.start(A3, ac_ref)
            bank.start(A2, acsw_ref)

        x12(X12)
        x1(X1)
        x2(X2)
        bank.start(A, a_ref)
        bank.wait(A3, A2, X12)
        a3 = split(bank.get(A3))
        moved = bank.get(A2) - mm(a3, bank.get(X12))
        bank.wait(X1, A)
        res[...] = bank.get(A) - mm(a3, bank.get(X1))
        bank.wait(X2)
        res[...] -= mm(moved, bank.get(X2))

    @pl.when((row >= 2) & (xl == 1) & (core == 0))
    def _():
        bank.start(A3, asw_ref)
        x1(X1)
        bank.start(A, a_ref)
        x2(X2)
        bank.wait(A3, X1, A)
        moved = bank.get(A) - mm(bank.get(A3), bank.get(X1))
        bank.wait(X2)
        res[...] = mm(moved, bank.get(X2))

    @pl.when((row >= 2) & (xl == 1) & (core == 1))
    def _():
        bank.start(A, a_ref)
        x1(X1)
        bank.wait(A, X1)
        res[...] = mm(bank.get(A), bank.get(X1))

    @pl.when((row == 1) & (xl == 0))
    def _():
        bank.start(INV, inv_ref)

        @pl.when(core == 0)
        def _():
            bank.start(L1, ac_ref)

        @pl.when(core == 1)
        def _():
            bank.start(L1, acsw_ref)

        join(bank, W, core, w_ref, wsw_ref)
        x2(X2)
        join(bank, SYM, core, one_ref, onesw_ref)
        bank.start(XOWN, x_ref)
        rows_of(bank, T, ts_ref, 0, N)
        bank.start(A, a_ref)
        bank.wait(INV, L1, W)
        inv = split(bank.get(INV))
        ap = bank.get(L1) - mm(inv, bank.get(W), ta=True)
        bank.wait(X2)
        side = mm(ap, bank.get(X2))
        bank.wait(SYM, XOWN)
        inner = 2.0 * mm(sym_half(bank.get(SYM)), bank.get(XOWN))
        bank.wait(T, A)
        res[...] = bank.get(A) - side - mm(inv, inner + bank.get(T), ta=True)

    @pl.when((row == 0) & (xl == 0))
    def _():
        x12(X12)
        rows_of(bank, T, ts_ref, 0, N)
        join(bank, W, core, wz_ref, wzsw_ref)
        x1(X1)
        rows_of(bank, X2, ts_ref, N, N)
        join(bank, L1, core, p_ref, psw_ref)
        bank.start(XOWN, x_ref)
        bank.start(INV, inv_ref)
        bank.start(A, a_ref)
        bank.wait(X12, T)
        inner = mm(bank.get(X12), bank.get(T), ta=True)
        bank.wait(W, X1)
        inner = inner + mm(bank.get(W), bank.get(X1), ta=True)
        bank.wait(L1, XOWN, X2)
        inner = bank.get(X2) - inner + 2.0 * mm(sym_half(bank.get(L1)), bank.get(XOWN))
        bank.wait(INV, A)
        res[...] = bank.get(A) - mm(bank.get(INV), inner, ta=True)

    @pl.when((row == 1) & (xl == 1) & (core == 0))
    def _():
        join(bank, A, core, ap_ref, apsw_ref)
        x2(X2)
        bank.wait(A, X2)
        res[...] = mm(bank.get(A), bank.get(X2))

    def end(here, there):
        join(bank, SYM, core, here, there)
        bank.start(INV, invo_ref)
        bank.wait(SYM, INV)
        inv = split(bank.get(INV))
        res[...] = mm(inv, mm(sym_half(bank.get(SYM)), inv), ta=True)

    @pl.when((row == 1) & (xl == 1) & (core == 1))
    def _():
        end(p1_ref, p1sw_ref)

    @pl.when((row == 0) & (xl == 1) & (core == 0))
    def _():
        end(p2_ref, p2sw_ref)

    @pl.when((row == 0) & (xl == 1) & (core == 1))
    def _():
        bank.start(A, a_ref)
        bank.wait(A)
        res[...] = bank.get(A)


def move(x, pairs):
    return lax.ppermute(x, ALL, [(dev(*a), dev(*b)) for a, b in pairs])


def exchange_cores(x, rows, columns):
    return move(x, [((r, c), (r, c ^ 1)) for r in rows for c in columns])


def swap_xh(x):
    return lax.ppermute(x, "xh", [(0, 1), (1, 0)])


def every(x):
    return lax.all_to_all(x, PLANE, 0, 0, tiled=True)


def local(low, adj):
    rows = range(32)
    below = range(2, 32)
    y, xh, z = (lax.axis_index(n) for n in ("y", "xh", "z"))
    xl, core = lax.axis_index("xl"), lax.axis_index("core")
    pos = jnp.stack([y * 8 + xh * 4 + z, xl, core, z]).astype(jnp.int32)
    tile, half = (N, N), (N, H)
    after = lax.optimization_barrier

    adj_sw = exchange_cores(adj, rows, (2, 3))
    low_sw = exchange_cores(low, rows, (2, 3))
    kq = move(low, [((1, 3), (1, 1)), ((0, 2), (0, 0)), ((1, 2), (1, 0))])

    sums_odd, = call(k_sum_odd, [(16, 32, N + H)], pos, adj, adj_sw, low, low_sw, slots=4)
    got = every(sums_odd)
    ac = move(adj, [((r, c), (r, c - 2)) for r in below for c in (2, 3)] + [((1, 2), (1, 0))])

    inv_odd, x12 = call(k_first, [tile, tile], pos, low, low_sw, slots=2, only=odd_top)
    kq, inv_odd = after((kq, inv_odd))
    kq_sw = exchange_cores(kq, (0, 1), (0, 1))
    inv, x, send_x = call(
        k_second, [tile, tile, (16, 32, N + H)], pos, low, kq, kq_sw, inv_odd, x12, slots=3)
    x12_zero = move(x12, [((1, 2), (0, 2))])
    x12_zero_sw = exchange_cores(x12_zero, (0,), (2,))
    got, send_x = after((got, send_x))
    got_x = every(send_x)

    part = jnp.sum(got, axis=0)
    other = swap_xh(part)
    ac, send_x = after((ac, send_x))
    ac_sw = exchange_cores(ac, range(1, 32), (0, 1))
    send, = call(k_send, [(16, 32, 2 * N)], pos, ac, ac_sw, low, part, other, slots=3, near=(4, 5))
    send, got_x = after((send, got_x))
    sums = every(send)
    xs = jnp.concatenate([got_x[0, :, :N], got_x[1]], 1)
    spread, = call(
        k_spread, [(16, 32, 2 * N + H)], xs, lax.ppermute(xs, "xh", [(0, 1)]), near=(0, 1))
    sums, spread, x12_zero_sw = after((sums, spread, x12_zero_sw))
    xs = every(spread)

    p1, = call(k_one_p, [half], pos, sums, adj, adj_sw, low, low_sw, inv_odd, slots=4, only=odd_one)
    p1_zero = move(p1, [((1, c), (0, c)) for c in (2, 3)])
    p1_one = move(p1, [((1, 2), (1, 0)), ((1, 3), (1, 1))])
    p1_sw = exchange_cores(p1, (1,), (2, 3))

    sums_own, p1 = after((sums, p1))
    own, = call(k_own, [(32, 2 * N)], sums_own, near=(0,))
    send, = call(
        k_spread, [(16, 32, 2 * N)], own, lax.ppermute(own, "xh", [(1, 0)]), near=(0, 1))
    ts = every(send)

    t12 = sums[:, :, H:N]
    t12_sw = exchange_cores(t12, (0,), (2, 3))
    base, = call(
        k_zero_base, [half], pos, sums, t12, t12_sw, adj, adj_sw, inv_odd, x12_zero, x12_zero_sw,
        slots=5, only=odd_zero)
    w1, ap = call(
        k_one_w, [half, half], pos, sums, p1, p1_sw, adj, adj_sw, inv_odd, x12, slots=5, only=odd_one)
    w_one = move(w1, [((1, 2), (1, 0)), ((1, 3), (1, 1))])

    p1_zero, base, send = after((p1_zero, base, send))
    p1_zero_sw = exchange_cores(p1_zero, (0,), (2, 3))
    w0, = call(
        k_zero_w, [half], pos, sums, p1_zero, p1_zero_sw, x12_zero, x12_zero_sw, slots=3, only=odd_zero)
    w_zero = move(w0, [((0, 2), (0, 0)), ((0, 3), (0, 1))])
    p2, = call(
        k_zero_p, [half], pos, base, w0, x12_zero, x12_zero_sw, inv_odd, low, low_sw, slots=5, only=odd_zero)
    p2_zero = move(p2, [((0, 2), (0, 0)), ((0, 3), (0, 1))])
    p2_sw = exchange_cores(p2, (0,), (3,))
    ap_sw = exchange_cores(ap, (1,), (3,))

    p1_one_sw = exchange_cores(p1_one, (1,), (0, 1))
    w_one_sw = exchange_cores(w_one, (1,), (0, 1))
    xs_sw = exchange_cores(xs[:, :, 2 * N:], rows, (0, 1))
    w_zero, xs_sw, p1_one_sw = after((w_zero, xs_sw, p1_one_sw))
    w_zero_sw = exchange_cores(w_zero, (0,), (0, 1))
    p2_zero, w_zero_sw = after((p2_zero, w_zero_sw))
    p2_zero_sw = exchange_cores(p2_zero, (0,), (0, 1))
    out, = call(
        k_final, [adj.shape], pos, adj, adj_sw, ac, ac_sw, xs, xs_sw, ts, inv, x,
        p1_one, p1_one_sw, w_one, w_one_sw, w_zero, w_zero_sw, p2_zero, p2_zero_sw, ap, ap_sw,
        p1, p1_sw, p2, p2_sw, inv_odd, slots=9)
    return out


def solution(mesh):
    fine = Mesh(mesh.devices.reshape(4, 2, 4, 2, 2), ALL)
    placed = P(None, ("y", "xh", "z"), None, ("xl", "core"))
    return jax.shard_map(
        local, mesh=fine, in_specs=(placed, placed), out_specs=placed, check_vma=False
    )
```
